256 devices in a mesh: tmpl: 32 (over x, y, core), chan: 8 (over z).
Axes of the slice: x: 4, y: 4, z: 8, core: 2. Of those that a mesh axis runs over, the one named last changes fastest.
Arguments:
- record: float32 [1024, 12288], P(None, ('tmpl', 'chan')), as said below
- channel_order: int32 [1024], replicated, may hold values from 0 to 1023, each once
- templates: float32 [256, 30, 600], P('tmpl'), as said below
- group_of_slot: int32 [256, 30, 1], replicated, may hold values from 0 to 7; in each aligned block of 240 rows (0 to 239, 240 to 479, ..., all dimensions but the last counted through in order) at most 60 rows name the same one
- place_of_slot: int32 [256, 30], replicated, may hold values from 0 to 127
Outputs:
- stack: float32 [256, 12288], P('tmpl', 'chan')
The draws below stay inside these ranges and needn't reach their ends.
Inputs may be any that keep to these rules, and one draw needn't show every extreme that they name: Channels channel_order[g * 128] to channel_order[(g + 1) * 128 - 1] form channel group g. `group_of_slot`: among the 240 slots of one template block, at most 60 name the same channel group. `record`: real samples. `templates`: real samples.
All inputs are finite; a program needn't handle non-finite values.
Results may differ from the reference program's by a relative error of at most 0.000098.
Values sent between devices are 32-bit elements; how exact they have to be, the bound alone decides.
No kernel may reach another device: no remote copies, remote signals or barrier semaphores. Data moves between devices by JAX's collectives and lax.ppermute only.
A program may use at most 128 MiB of HBM per device.

```python
import math
import jax
import jax.numpy as jnp
import numpy as np
from jax import lax

GROUP_CHANNELS = 128
BLOCK_TEMPLATES = 8
SLOTS_PER_TMPL = 30
PATTERN_SAMPLES = 600
CHANNEL_COUNT = 1024
TEMPLATE_COUNT = 256
TRACE_SAMPLES = 12288
MOST_BLOCK_SLOTS = 60


def draw_record(key, part):
    key = jax.random.fold_in(key, 17)
    amplitude_seed, disturbance_seed, pulse_seed = jax.random.split(key, 3)
    channel_gain = jnp.exp(jax.random.uniform(amplitude_seed, (CHANNEL_COUNT, 1), jnp.float32, 0.0, jnp.log(10.0)))
    background = jnp.clip(jax.random.normal(disturbance_seed, (CHANNEL_COUNT, TRACE_SAMPLES), jnp.float32), -6.0, 6.0)
    pulse_outline = 1.0 + 0.0 * jax.random.uniform(pulse_seed, (1, TRACE_SAMPLES), jnp.float32)
    return background * channel_gain * pulse_outline


def draw_templates(key, part):
    key = jax.random.fold_in(key, 29)
    scale_key, wave_key = jax.random.split(key, 2)
    gain_per_slot = jnp.exp(jax.random.uniform(scale_key, (TEMPLATE_COUNT, SLOTS_PER_TMPL, 1), jnp.float32, jnp.log(0.3), jnp.log(3.0)))
    signal_waveform = jnp.clip(jax.random.normal(wave_key, (TEMPLATE_COUNT, SLOTS_PER_TMPL, PATTERN_SAMPLES), jnp.float32), -6.0, 6.0)
    return signal_waveform * gain_per_slot


def place_ends(values, stream_key, least, high):
    extent = values.shape
    place = [jax.random.randint(jax.random.fold_in(stream_key, axis), (), 0, extent[axis]) for axis in range(len(extent))]
    values = values.at[tuple(place)].set(least)
    longest = extent.index(max(extent))
    place[longest] = (place[longest] + 1) % extent[longest]
    return values.at[tuple(place)].set(high)


def deal_out(stream_key, own, number, rows, amount, top, most, lean):
    order = jax.random.permutation(stream_key, amount)
    heavy_load, ordinary = shares(amount, rows * top, most, lean, True), shares(amount, rows * top, most, lean, False)
    places = jnp.arange(amount)

    def named(lengths, turn):
        used = int((lengths > 0).sum())
        fixed = max(1, used // 4)
        moved = fixed + (places - fixed + turn * (used - fixed)) % max(1, amount - fixed)
        return jnp.zeros((amount,), jnp.int32).at[order[jnp.where(places < fixed, places, moved)]].set(jnp.asarray(lengths, jnp.int32))

    lengths = jnp.where(number % 4 == 0, named(heavy_load, number // 4), named(ordinary, number - number // 4 - 1))
    mixed = jax.random.permutation(jax.random.fold_in(own, 3), amount)
    donor, taker = mixed[0:amount // 2 * 2:2], mixed[1:amount // 2 * 2:2]
    margin = jnp.minimum(lengths[donor] - 1, most - lengths[taker]) // 2
    margin = jnp.where((donor == order[0]) | (taker == order[0]) | (lengths[taker] == 0), 0, jnp.maximum(margin, 0))
    moved = jax.random.randint(jax.random.fold_in(own, 4), (amount // 2,), 0, 1 << 20) % (margin + 1)
    lengths = lengths.at[donor].add(-moved).at[taker].add(moved)
    members = jnp.searchsorted(jnp.cumsum(lengths), jnp.arange(rows * top), side="right").astype(jnp.int32)
    grid = members.reshape(top, rows).T
    grid = grid[jax.random.permutation(jax.random.fold_in(own, 1), rows)]
    turn = jax.random.randint(jax.random.fold_in(own, 2), (rows, 1), 0, top)
    return jnp.take_along_axis(grid, (jnp.arange(top)[None, :] + turn) % top, axis=1)


def shares(number_of, total, most, skew, full):
    portions = [(1 << 20) // math.isqrt(standing ** skew) + 1 for standing in range(1, number_of + 1)]
    largest = most if full else min(most, max(-(-total // number_of), total * portions[0] // sum(portions)))
    least = 1 if total - largest >= number_of - 1 else 0
    holding, spare = [largest] + [least] * (number_of - 1), total - largest - least * (number_of - 1)
    while spare > 0:
        free = [i for i in range(1, number_of) if holding[i] < largest] or [i for i in range(1, number_of) if holding[i] < most]
        mass, budget = sum([portions[i] for i in free]), spare
        for i in free:
            addition = min(most - holding[i], max(1, budget * portions[i] // mass), spare)
            holding[i] = holding[i] + addition
            spare = spare - addition
    return np.array(holding)


def setup_inputs(seed: int = 0) -> dict:
    key_of = jax.random.split(jax.random.key(seed), 6)
    record = draw_record(jax.random.fold_in(key_of[5], 71), 0)
    channel_order = jax.random.permutation(key_of[1], CHANNEL_COUNT).astype(jnp.int32)
    templates = draw_templates(jax.random.fold_in(key_of[5], 71), 0)
    group_of_slot_keys = jax.random.split(jax.random.fold_in(key_of[3], 1), TEMPLATE_COUNT * SLOTS_PER_TMPL // (BLOCK_TEMPLATES * SLOTS_PER_TMPL))
    group_of_slot_turns = jax.random.permutation(jax.random.fold_in(key_of[3], 3), TEMPLATE_COUNT * SLOTS_PER_TMPL // (BLOCK_TEMPLATES * SLOTS_PER_TMPL))
    group_of_slot = jax.vmap(lambda own, number: deal_out(jax.random.fold_in(key_of[3], 2), own, number, BLOCK_TEMPLATES * SLOTS_PER_TMPL, CHANNEL_COUNT // GROUP_CHANNELS, 1, MOST_BLOCK_SLOTS, 2))(group_of_slot_keys, group_of_slot_turns).reshape((TEMPLATE_COUNT, SLOTS_PER_TMPL, 1))
    place_of_slot = place_ends(jax.random.randint(key_of[4], (TEMPLATE_COUNT, SLOTS_PER_TMPL), 0, GROUP_CHANNELS), jax.random.fold_in(key_of[4], 1), 0, GROUP_CHANNELS - 1).astype(jnp.int32)
    return {"record": record, "channel_order": channel_order, "templates": templates, "group_of_slot": group_of_slot, "place_of_slot": place_of_slot}


def reference(record, channel_order, templates, group_of_slot, place_of_slot):
    chan_ids = channel_order[group_of_slot[:, :, 0] * GROUP_CHANNELS + place_of_slot].astype(jnp.int32)
    squares = record * record
    wrapped = jnp.concatenate([squares, squares[:, :PATTERN_SAMPLES - 1]], axis=1)
    window_sum = lax.reduce_window(wrapped, jnp.float32(0), lax.add, (1, PATTERN_SAMPLES), (1, 1), 'VALID')
    energy = jnp.sqrt(window_sum / PATTERN_SAMPLES + 1e-06)
    template_norm = jnp.sqrt(lax.optimization_barrier(jnp.mean(templates * templates, axis=2)) + 1e-06)
    scale_per_slot = 1.0 / (jnp.sqrt(jnp.float32(PATTERN_SAMPLES * SLOTS_PER_TMPL)) * template_norm)

    def one_template(pattern_entry):
        template_wave, chan_rows, weight = pattern_entry
        traces = record[chan_rows]
        padded_record = jnp.zeros((SLOTS_PER_TMPL, TRACE_SAMPLES), jnp.float32).at[:, :PATTERN_SAMPLES].set(template_wave)
        cross_spec = jnp.conj(jnp.fft.rfft(padded_record, axis=1)) * jnp.fft.rfft(traces, axis=1)
        correlation = jnp.fft.irfft(cross_spec, n=TRACE_SAMPLES, axis=1)
        return lax.optimization_barrier(jnp.sum(correlation * weight[:, None] / energy[chan_rows], axis=0))
    return lax.map(one_template, (templates, chan_ids, scale_per_slot))
```

```python
import jax
import jax.numpy as jnp
import ml_dtypes
import numpy as np
from jax import lax
from jax.experimental import pallas as pl
from jax.experimental.pallas import tpu as pltpu
from jax.sharding import PartitionSpec as P

SLOTS = 30
TAPS = 600
BLOCK = 8
LANES = 256
USED = SLOTS * BLOCK
HALF = 512
HOP = 384
GROUP = 128

F32 = jnp.float32
BF16 = jnp.bfloat16


def split_np(table):
    hi = table.astype(ml_dtypes.bfloat16)
    lo = (table - hi.astype(np.float64)).astype(ml_dtypes.bfloat16)
    return hi, lo


def tables():
    n = np.arange(HALF, dtype=np.int64)
    m = np.arange(HALF // 2, dtype=np.int64)
    even = (m[:, None] * n[None, :] % HALF) * (2 * np.pi / HALF)
    odd = ((2 * m[:, None] + 1) * n[None, :] % (2 * HALF)) * (np.pi / HALF)
    even_imag = -np.sin(even)
    even_imag[0] = 1.0 - 2.0 * (n % 2)
    f_even = np.concatenate([np.cos(even), even_imag])
    f_odd = np.concatenate([np.cos(odd), -np.sin(odd)])
    weight = np.full((HALF // 2, 1), 2.0 / HALF)
    weight[0] = 1.0 / HALF
    weight = np.concatenate([weight, weight])
    inv_even = 0.5 * weight * f_even
    inv_odd = (1.0 / HALF) * f_odd
    inverse = np.concatenate([inv_even, inv_odd])[:, :HOP].T
    out = []
    for table in (f_even, f_odd, inverse):
        hi, lo = split_np(table)
        out.append(np.concatenate([hi, hi, lo], axis=1))
    return out


def split(value):
    hi = value.astype(BF16)
    lo = (value - hi.astype(F32)).astype(BF16)
    return hi, lo


def dot3(table_ref, value):
    hi, lo = split(value)
    return jnp.dot(table_ref[...], jnp.concatenate([hi, lo, hi], axis=0), preferred_element_type=F32)


def template_kernel(waves_ref, f_even_ref, f_odd_ref, er_ref, ei_ref, en_ref, odd_ref, pad_ref):
    pad_ref[...] = jnp.zeros_like(pad_ref)
    pad_ref[:USED, :TAPS] = waves_ref[...]
    waves = pad_ref[...].T
    mean = jnp.sum(waves * waves, axis=0, keepdims=True) * (1.0 / TAPS)
    scale = 1.0 / (jnp.sqrt(mean + 1e-6) * np.float32(np.sqrt(TAPS * SLOTS)))
    waves = waves * scale
    head, tail = waves[:HALF], waves[HALF:]
    tail = jnp.concatenate([tail, jnp.zeros((HALF - tail.shape[0], LANES), F32)], axis=0)
    even = dot3(f_even_ref, head + tail)
    odd_ref[...] = dot3(f_odd_ref, head - tail)
    real, imag = even[: HALF // 2], even[HALF // 2 :]
    first = lax.broadcasted_iota(jnp.int32, real.shape, 0) == 0
    er_ref[...] = real
    ei_ref[...] = jnp.where(first, 0.0, imag)
    en_ref[...] = jnp.where(first, imag, real)


def lane_pick(source, index):
    return jnp.take_along_axis(source, index, axis=1)


def select_kernel(record_ref, order_ref, group_ref, place_ref, out_ref, chan_ref):
    groups = order_ref.shape[0]
    blocks = group_ref.shape[0]
    span = record_ref.shape[0]
    for row in range(0, blocks, 8):
        for col in range(0, LANES, GROUP):
            group = group_ref[row : row + 8, col : col + GROUP]
            place = place_ref[row : row + 8, col : col + GROUP]
            chan = jnp.zeros_like(place)
            for g in range(groups):
                names = jnp.broadcast_to(order_ref[g : g + 1, :], (8, GROUP))
                chan = jnp.where(group == g, lane_pick(names, place), chan)
            for i in range(8):
                one = jnp.broadcast_to(chan[i : i + 1], (8, GROUP))
                chan_ref[row + i, :, col : col + GROUP] = one

    def one_block(block, _):
        for col in range(0, LANES, GROUP):
            chan = chan_ref[block, :, col : col + GROUP]
            high = lax.shift_right_logical(chan, 7)
            low = jnp.bitwise_and(chan, GROUP - 1)
            for row in range(0, span, 8):
                acc = jnp.zeros((8, GROUP), F32)
                for g in range(groups):
                    picked = lane_pick(record_ref[row : row + 8, g * GROUP : (g + 1) * GROUP], low)
                    acc = jnp.where(high == g, picked, acc)
                out_ref[block, row : row + 8, col : col + GROUP] = acc
        return 0

    lax.fori_loop(0, blocks, one_block, 0)


def source_of(block):
    lane, z = divmod(block, 8)
    return lane * 8 + (z % 4) * 2 + z // 4


def halo_kernel(recv_ref, halo_ref):
    span = recv_ref.shape[1]
    rows = halo_ref.shape[0]
    for block in range(-(-rows // span)):
        count = min(span, rows - block * span)
        halo_ref[block * span : block * span + count, :] = recv_ref[source_of(block), :count, :]


def segments(x_ref, sq_ref, first, count, specs, f_even_ref, f_odd_ref, inv_ref, out_ref):
    er_ref, ei_ref, en_ref, odd_ref = specs
    quarter = HALF // 2
    lags = count * HOP
    rows = lags + TAPS
    sq = x_ref[:rows] * x_ref[:rows]
    for step in (1, 2, 4):
        sq_ref[:rows] = sq
        sq_ref[rows : rows + 8] = jnp.zeros((8, LANES), F32)
        sq = sq_ref[:rows] + sq_ref[step : rows + step]
    total = sq[74 * 8 : 74 * 8 + lags]
    length = 1
    have = rows
    at = {64: 0, 8: 64, 2: 72}
    while length < 64:
        have = have - 8 * length
        sq = sq[:have] + sq[8 * length : 8 * length + have]
        length *= 2
        if length in at:
            total = total + sq[8 * at[length] : 8 * at[length] + lags]
    scale = lax.rsqrt(total * (1.0 / TAPS) + 1e-6)
    for seg in range(count):
        base = seg * HOP
        head, tail = x_ref[base : base + HALF], x_ref[base + HALF : base + 2 * HALF]
        even = dot3(f_even_ref, head + tail)
        odd = dot3(f_odd_ref, head - tail)
        re, im = even[:quarter], even[quarter:]
        ro, io = odd[:quarter], odd[quarter:]
        tr, ti, tn = er_ref[...], ei_ref[...], en_ref[...]
        to, tp = odd_ref[:quarter], odd_ref[quarter:]
        product = jnp.concatenate(
            [re * tr + im * ti, im * tn - re * ti, ro * to + io * tp, io * to - ro * tp], axis=0
        )
        corr = dot3(inv_ref, product) * scale[base : base + HOP]
        folded = (corr[:, :GROUP] + corr[:, GROUP:]).T
        acc = folded[:BLOCK]
        for s in range(1, GROUP // BLOCK):
            acc = acc + folded[s * BLOCK : (s + 1) * BLOCK]
        out_ref[:, (first + seg) * HOP : (first + seg + 1) * HOP] = acc


def near_kernel(recv_ref, er, ei, en, od, fe, fo, inv, out_ref, x_ref, sq_ref):
    span = recv_ref.shape[1]
    for block in range(x_ref.shape[0] // span):
        x_ref[block * span : (block + 1) * span, :] = recv_ref[source_of(block)]
    out_ref[...] = jnp.zeros_like(out_ref)
    segments(x_ref, sq_ref, 0, 2, (er, ei, en, od), fe, fo, inv, out_ref)


def far_kernel(near_ref, recv_ref, halo_ref, er, ei, en, od, fe, fo, inv, out_ref, x_ref, sq_ref):
    span = recv_ref.shape[1]
    start = 2 * HOP
    blocks = recv_ref.shape[0]
    skip = start // span
    for block in range(skip, blocks):
        x_ref[(block - skip) * span : (block - skip + 1) * span, :] = recv_ref[source_of(block)]
    here = (blocks - skip) * span
    rows = halo_ref.shape[0]
    x_ref[here : here + rows, :] = halo_ref[...]
    x_ref[here + rows :, :] = jnp.zeros((x_ref.shape[0] - here - rows, LANES), F32)
    out_ref[:, :start] = near_ref[:, :start]
    segments(x_ref, sq_ref, 2, 2, (er, ei, en, od), fe, fo, inv, out_ref)


def call(kernel, out_shape, scratch, flops, nbytes, mib, name):
    return pl.pallas_call(
        kernel,
        out_shape=out_shape,
        scratch_shapes=scratch,
        compiler_params=pltpu.CompilerParams(vmem_limit_bytes=mib << 20),
        cost_estimate=pl.CostEstimate(flops=flops, bytes_accessed=nbytes, transcendentals=0),
        name=name,
    )


def by_block(slots, blocks):
    slots = slots.reshape(blocks, BLOCK, SLOTS).transpose(0, 2, 1).reshape(blocks, USED)
    return jnp.pad(slots, ((0, 0), (0, LANES - USED)))


def shards(record, channel_order, templates, group_of_slot, place_of_slot):
    blocks = lax.axis_size("tmpl")
    planes = lax.axis_size("chan")
    span = record.shape[1]
    lags = blocks * span
    f_even, f_odd, inverse = (jnp.asarray(t) for t in tables())
    moves = []
    for b in range(blocks):
        for z in range(planes):
            plane, lane = divmod(b, blocks // planes)
            moves.append((b * planes + z, source_of(lane * 8 + z) * planes + plane))
    raw = lax.ppermute(record.T, ("tmpl", "chan"), moves)

    waves = templates.transpose(1, 0, 2).reshape(USED, TAPS)
    quarter = jax.ShapeDtypeStruct((HALF // 2, LANES), F32)
    specs = call(
        template_kernel,
        (quarter, quarter, quarter, jax.ShapeDtypeStruct((HALF, LANES), F32)),
        [pltpu.VMEM((LANES, 640), F32)],
        2 * 3 * HALF * 2 * HALF * LANES,
        6 << 20,
        48,
        "template_spectra",
    )(waves, f_even, f_odd)

    sent = call(
        select_kernel,
        jax.ShapeDtypeStruct((blocks, span, LANES), F32),
        [pltpu.VMEM((blocks, 8, LANES), jnp.int32)],
        1 << 20,
        4 << 20,
        48,
        "select_channels",
    )(
        raw,
        channel_order.reshape(-1, GROUP),
        by_block(group_of_slot, blocks),
        by_block(place_of_slot, blocks),
    )
    recv = lax.all_to_all(sent, "tmpl", split_axis=0, concat_axis=0, tiled=True)
    head = call(
        halo_kernel, jax.ShapeDtypeStruct((TAPS, LANES), F32), [], 0, 1 << 20, 48, "halo"
    )(recv)
    halo = lax.ppermute(head, "chan", [((z + 1) % planes, z) for z in range(planes)])
    out = jax.ShapeDtypeStruct((BLOCK, lags), F32)
    scratch = [pltpu.VMEM((1536, LANES), F32), pltpu.VMEM((1536, LANES), F32)]
    flops = 2 * 2 * 3 * (2 * HALF * HALF + HOP * 2 * HALF) * LANES
    near = call(near_kernel, out, scratch, flops, 6 << 20, 56, "near_segments")(
        recv, *specs, f_even, f_odd, inverse
    )
    return call(far_kernel, out, scratch, flops, 6 << 20, 56, "far_segments")(
        near, recv, halo, *specs, f_even, f_odd, inverse
    )


def solution(mesh):
    placed = (P(None, ("tmpl", "chan")), P(), P("tmpl", None, None), P(), P())
    return jax.shard_map(
        shards, mesh=mesh, in_specs=placed, out_specs=P("tmpl", "chan"), check_vma=False
    )
```

```python
import jax
import jax.numpy as jnp
import ml_dtypes
import numpy as np
from jax import lax
from jax.experimental import pallas as pl
from jax.experimental.pallas import tpu as pltpu
from jax.sharding import PartitionSpec as P

SLOTS = 30
TAPS = 600
BLOCK = 8
LANES = 256
USED = SLOTS * BLOCK
HALF = 512
HOP = 384
GROUP = 128
BACK = 304
NEXT = 296

F32 = jnp.float32
BF16 = jnp.bfloat16


def split_np(table):
    hi = table.astype(ml_dtypes.bfloat16)
    lo = (table - hi.astype(np.float64)).astype(ml_dtypes.bfloat16)
    return hi, lo


def tables():
    n = np.arange(HALF, dtype=np.int64)
    m = np.arange(HALF // 2, dtype=np.int64)
    even = (m[:, None] * n[None, :] % HALF) * (2 * np.pi / HALF)
    odd = ((2 * m[:, None] + 1) * n[None, :] % (2 * HALF)) * (np.pi / HALF)
    even_imag = -np.sin(even)
    even_imag[0] = 1.0 - 2.0 * (n % 2)
    f_even = np.concatenate([np.cos(even), even_imag])
    f_odd = np.concatenate([np.cos(odd), -np.sin(odd)])
    weight = np.full((HALF // 2, 1), 2.0 / HALF)
    weight[0] = 1.0 / HALF
    weight = np.concatenate([weight, weight])
    inv_even = 0.5 * weight * f_even
    inv_odd = (1.0 / HALF) * f_odd
    inverse = np.concatenate([inv_even, inv_odd])[:, :HOP].T
    out = []
    for table in (f_even, f_odd, inverse):
        hi, lo = split_np(table)
        out.append(np.concatenate([hi, hi, lo], axis=1))
    return out


def split(value):
    hi = value.astype(BF16)
    lo = (value - hi.astype(F32)).astype(BF16)
    return hi, lo


def dot3(table_ref, value):
    hi, lo = split(value)
    return jnp.dot(table_ref[...], jnp.concatenate([hi, lo, hi], axis=0), preferred_element_type=F32)


def template_kernel(waves_ref, f_even_ref, f_odd_ref, er_ref, ei_ref, en_ref, odd_ref, pad_ref):
    pad_ref[...] = jnp.zeros_like(pad_ref)
    pad_ref[:USED, :TAPS] = waves_ref[...]
    waves = pad_ref[...].T
    mean = jnp.sum(waves * waves, axis=0, keepdims=True) * (1.0 / TAPS)
    scale = 1.0 / (jnp.sqrt(mean + 1e-6) * np.float32(np.sqrt(TAPS * SLOTS)))
    waves = waves * scale
    head, tail = waves[:HALF], waves[HALF:]
    tail = jnp.concatenate([tail, jnp.zeros((HALF - tail.shape[0], LANES), F32)], axis=0)
    even = dot3(f_even_ref, head + tail)
    odd_ref[...] = dot3(f_odd_ref, head - tail)
    real, imag = even[: HALF // 2], even[HALF // 2 :]
    first = lax.broadcasted_iota(jnp.int32, real.shape, 0) == 0
    er_ref[...] = real
    ei_ref[...] = jnp.where(first, 0.0, imag)
    en_ref[...] = jnp.where(first, imag, real)


def lane_pick(source, index):
    return jnp.take_along_axis(source, index, axis=1)


def select_kernel(record_ref, order_ref, group_ref, place_ref, out_ref, chan_ref):
    groups = order_ref.shape[0]
    blocks = group_ref.shape[0]
    span = record_ref.shape[0]
    for row in range(0, blocks, 8):
        for col in range(0, LANES, GROUP):
            group = group_ref[row : row + 8, col : col + GROUP]
            place = place_ref[row : row + 8, col : col + GROUP]
            chan = jnp.zeros_like(place)
            for g in range(groups):
                names = jnp.broadcast_to(order_ref[g : g + 1, :], (8, GROUP))
                chan = jnp.where(group == g, lane_pick(names, place), chan)
            for i in range(8):
                one = jnp.broadcast_to(chan[i : i + 1], (8, GROUP))
                chan_ref[row + i, :, col : col + GROUP] = one

    def one_block(block, _):
        for col in range(0, LANES, GROUP):
            chan = chan_ref[block, :, col : col + GROUP]
            high = lax.shift_right_logical(chan, 7)
            low = jnp.bitwise_and(chan, GROUP - 1)
            for row in range(0, span, 8):
                acc = jnp.zeros((8, GROUP), F32)
                for g in range(groups):
                    picked = lane_pick(record_ref[row : row + 8, g * GROUP : (g + 1) * GROUP], low)
                    acc = jnp.where(high == g, picked, acc)
                out_ref[block, row : row + 8, col : col + GROUP] = acc
        return 0

    lax.fori_loop(0, blocks, one_block, 0)


def route(block, plane):
    low, core, z = block // 16, block // 8 % 2, block % 8
    key = z ^ (5 * core)
    return (plane ^ key) * 4 + (low ^ (key & 1)) * 2 + core


def load_rows(recv_ref, plane, x_ref, first, count, at):
    span = recv_ref.shape[1]
    row = first
    while row < first + count:
        block, low = divmod(row, span)
        take = min(span - low, first + count - row)
        x_ref[at : at + take, :] = recv_ref[route(block, plane), low : low + take, :]
        row += take
        at += take


def ends_kernel(plane_ref, recv_ref, head_ref, tail_ref):
    plane = plane_ref[0]
    total = recv_ref.shape[0] * recv_ref.shape[1]
    load_rows(recv_ref, plane, head_ref, 0, NEXT, 0)
    load_rows(recv_ref, plane, tail_ref, total - BACK, BACK, 0)


def segments(x_ref, sq_ref, count, specs, f_even_ref, f_odd_ref, inv_ref):
    er_ref, ei_ref, en_ref, odd_ref = specs
    quarter = HALF // 2
    lags = count * HOP
    rows = lags + TAPS
    sq = x_ref[:rows] * x_ref[:rows]
    for step in (1, 2, 4):
        sq_ref[:rows] = sq
        sq_ref[rows : rows + 8] = jnp.zeros((8, LANES), F32)
        sq = sq_ref[:rows] + sq_ref[step : rows + step]
    total = sq[74 * 8 : 74 * 8 + lags]
    length = 1
    have = rows
    at = {64: 0, 8: 64, 2: 72}
    while length < 64:
        have = have - 8 * length
        sq = sq[:have] + sq[8 * length : 8 * length + have]
        length *= 2
        if length in at:
            total = total + sq[8 * at[length] : 8 * at[length] + lags]
    scale = lax.rsqrt(total * (1.0 / TAPS) + 1e-6)
    stacks = []
    for seg in range(count):
        base = seg * HOP
        head, tail = x_ref[base : base + HALF], x_ref[base + HALF : base + 2 * HALF]
        even = dot3(f_even_ref, head + tail)
        odd = dot3(f_odd_ref, head - tail)
        re, im = even[:quarter], even[quarter:]
        ro, io = odd[:quarter], odd[quarter:]
        tr, ti, tn = er_ref[...], ei_ref[...], en_ref[...]
        to, tp = odd_ref[:quarter], odd_ref[quarter:]
        product = jnp.concatenate(
            [re * tr + im * ti, im * tn - re * ti, ro * to + io * tp, io * to - ro * tp], axis=0
        )
        corr = dot3(inv_ref, product) * scale[base : base + HOP]
        folded = (corr[:, :GROUP] + corr[:, GROUP:]).T
        acc = folded[:BLOCK]
        for s in range(1, GROUP // BLOCK):
            acc = acc + folded[s * BLOCK : (s + 1) * BLOCK]
        stacks.append(acc)
    return stacks


def near_kernel(plane_ref, recv_ref, er, ei, en, od, fe, fo, inv, out_ref, x_ref, sq_ref):
    load_rows(recv_ref, plane_ref[0], x_ref, HOP - BACK, HOP + 2 * HALF, 0)
    one, two = segments(x_ref, sq_ref, 2, (er, ei, en, od), fe, fo, inv)
    out_ref[:, :HOP] = one
    out_ref[:, HOP:] = two


def back_kernel(plane_ref, recv_ref, tail_ref, er, ei, en, od, fe, fo, inv, out_ref, x_ref, sq_ref):
    x_ref[:BACK] = tail_ref[...]
    load_rows(recv_ref, plane_ref[0], x_ref, 0, 2 * HALF - BACK, BACK)
    (out_ref[...],) = segments(x_ref, sq_ref, 1, (er, ei, en, od), fe, fo, inv)


def last_kernel(plane_ref, recv_ref, head_ref, er, ei, en, od, fe, fo, inv, out_ref, x_ref, sq_ref):
    total = recv_ref.shape[0] * recv_ref.shape[1]
    first = 3 * HOP - BACK
    own = total - first
    load_rows(recv_ref, plane_ref[0], x_ref, first, own, 0)
    x_ref[own : own + NEXT] = head_ref[...]
    x_ref[own + NEXT : 2 * HALF] = jnp.zeros((2 * HALF - own - NEXT, LANES), F32)
    (out_ref[...],) = segments(x_ref, sq_ref, 1, (er, ei, en, od), fe, fo, inv)


def call(kernel, out_shape, scratch, flops, nbytes, mib, name, scalars=0):
    def run(*operands):
        smem = pl.BlockSpec(memory_space=pltpu.SMEM)
        vmem = pl.BlockSpec(memory_space=pltpu.VMEM)
        return pl.pallas_call(
            kernel,
            out_shape=out_shape,
            in_specs=[smem if i < scalars else vmem for i in range(len(operands))],
            scratch_shapes=scratch,
            compiler_params=pltpu.CompilerParams(vmem_limit_bytes=mib << 20),
            cost_estimate=pl.CostEstimate(flops=flops, bytes_accessed=nbytes, transcendentals=0),
            name=name,
        )(*operands)

    return run


def by_block(slots, blocks):
    slots = slots.reshape(blocks, BLOCK, SLOTS).transpose(0, 2, 1).reshape(blocks, USED)
    return jnp.pad(slots, ((0, 0), (0, LANES - USED)))


def shards(record, channel_order, templates, group_of_slot, place_of_slot):
    blocks = lax.axis_size("tmpl")
    planes = lax.axis_size("chan")
    span = record.shape[1]
    lags = blocks * span
    f_even, f_odd, inverse = (jnp.asarray(t) for t in tables())
    across, along = [], []
    per_plane = blocks // planes
    for b in range(blocks):
        for z in range(planes):
            plane, lane = divmod(b, per_plane)
            keeper = route(lane * planes + z, plane)
            across.append((b * planes + z, keeper * planes + z))
            along.append((keeper * planes + z, keeper * planes + plane))
    raw = lax.ppermute(record.T, ("tmpl", "chan"), across)
    raw = lax.ppermute(raw, ("tmpl", "chan"), along)
    plane = lax.axis_index("chan").astype(jnp.int32).reshape(1)

    waves = templates.transpose(1, 0, 2).reshape(USED, TAPS)
    quarter = jax.ShapeDtypeStruct((HALF // 2, LANES), F32)
    specs = call(
        template_kernel,
        (quarter, quarter, quarter, jax.ShapeDtypeStruct((HALF, LANES), F32)),
        [pltpu.VMEM((LANES, 640), F32)],
        2 * 3 * HALF * 2 * HALF * LANES,
        6 << 20,
        16,
        "template_spectra",
    )(waves, f_even, f_odd)

    group, place, plane, specs = lax.optimization_barrier(
        (by_block(group_of_slot, blocks), by_block(place_of_slot, blocks), plane, specs)
    )
    sent = call(
        select_kernel,
        jax.ShapeDtypeStruct((blocks, span, LANES), F32),
        [pltpu.VMEM((blocks, 8, LANES), jnp.int32)],
        1 << 20,
        4 << 20,
        8,
        "select_channels",
    )(raw, channel_order.reshape(-1, GROUP), group, place)
    recv = lax.all_to_all(sent, "tmpl", split_axis=0, concat_axis=0, tiled=True)
    rows = jax.ShapeDtypeStruct((BACK, LANES), F32), jax.ShapeDtypeStruct((NEXT, LANES), F32)
    head, tail = call(ends_kernel, rows[::-1], [], 0, 1 << 20, 8, "ends", 1)(plane, recv)
    up = [(z, (z + 1) % planes) for z in range(planes)]
    down = [(t, s) for s, t in up]
    after = lax.ppermute(head, "chan", down)
    before = lax.ppermute(tail, "chan", up)
    flops = 2 * 3 * (2 * HALF * HALF + HOP * 2 * HALF) * LANES
    shared = (*specs, f_even, f_odd, inverse)

    def part(kernel, count, name):
        lines = pltpu.VMEM(((count - 1) * HOP + 2 * HALF + 8, LANES), F32)
        shape = jax.ShapeDtypeStruct((BLOCK, count * HOP), F32)
        return call(kernel, shape, [lines, lines], count * flops, 8 << 20, 24, name, 1)

    middle = part(near_kernel, 2, "near_segments")(plane, recv, *shared)
    first = part(back_kernel, 1, "back_segment")(plane, recv, before, *shared)
    given = lax.ppermute(first[:, :BACK], "chan", down)
    last = part(last_kernel, 1, "last_segment")(plane, recv, after, *shared)
    return jnp.concatenate([first[:, BACK:], middle, last, given], axis=1)


def solution(mesh):
    placed = (P(None, ("tmpl", "chan")), P(), P("tmpl", None, None), P(), P())
    return jax.shard_map(
        shards, mesh=mesh, in_specs=placed, out_specs=P("tmpl", "chan"), check_vma=False
    )
```

```python
import jax
import jax.numpy as jnp
import ml_dtypes
import numpy as np
from jax import lax
from jax.experimental import pallas as pl
from jax.experimental.pallas import tpu as pltpu
from jax.sharding import PartitionSpec as P

SLOTS = 30
TAPS = 600
BLOCK = 8
LANES = 256
USED = SLOTS * BLOCK
HALF = 512
HOP = 384
MOST = 408
GROUP = 128
QUARTER = 256
ROOT = float(np.sqrt(2.0))
BACK = 232
KEEP = 128
NEXT = 368

F32 = jnp.float32
BF16 = jnp.bfloat16


def split_np(table):
    hi = table.astype(ml_dtypes.bfloat16)
    lo = (table - hi.astype(np.float64)).astype(ml_dtypes.bfloat16)
    return hi, lo


def tables():
    n = np.arange(QUARTER, dtype=np.int64)[None, :]
    m = np.arange(GROUP, dtype=np.int64)[:, None]
    forward, back = [], []
    for eighths in (0, 4, 1, 3):
        if eighths in (0, 4):
            angle = ((2 * m + eighths // 4) * n % (2 * QUARTER)) * (np.pi / QUARTER)
            imag = -np.sin(angle)
            weight = np.full((QUARTER, 1), 2.0 / QUARTER)
            if not eighths:
                imag[0] = 1.0 - 2.0 * (n[0] % 2)
                weight[0] = weight[GROUP] = 1.0 / QUARTER
            table = np.concatenate([np.cos(angle), imag])
            inverse = (weight * table).T
        else:
            angle = ((8 * m + eighths) * n % (8 * GROUP)) * (np.pi / (4 * GROUP))
            table = np.concatenate([np.cos(angle), -np.sin(angle)])
            sign = 1.0 if eighths == 1 else -1.0
            cos, sin = np.cos(angle[:, :GROUP]).T / GROUP, np.sin(angle[:, :GROUP]).T / GROUP
            root = np.sqrt(2.0)
            low = np.concatenate([cos + sign * sin, sign * cos - sin], axis=1)
            high = np.concatenate([-root * sin, -root * cos], axis=1)
            inverse = np.concatenate([low, high])
        forward.append(table)
        back.append(0.25 * inverse)
    out = []
    for stack in (forward, back):
        hi, lo = split_np(np.concatenate(stack))
        out.append(np.concatenate([hi, hi, lo], axis=1))
    return out


def split(value):
    hi = value.astype(BF16)
    lo = (value - hi.astype(F32)).astype(BF16)
    return hi, lo


def dot3(table_ref, part, value):
    hi, lo = split(value)
    both = jnp.concatenate([hi, lo, hi], axis=0)
    rows = table_ref[part * QUARTER : (part + 1) * QUARTER]
    return jnp.dot(rows, both, preferred_element_type=F32)


def transform(pieces, table_ref):
    one, two, three, four = pieces
    even, late = one + three, two + four
    odd, last = one - three, two - four
    third, fourth = last[:GROUP], last[GROUP:]
    plain = jnp.concatenate([odd[:GROUP] - third, odd[GROUP:] + fourth], axis=0)
    turned = ROOT * jnp.concatenate([fourth, -third], axis=0)
    residues = (even + late, even - late, plain - turned, plain + turned)
    return [dot3(table_ref, part, value) for part, value in enumerate(residues)]


def combine(parts):
    total, diff, left, right = parts
    plain = left + right
    turned = (left - right) * (1.0 / ROOT)
    third, fourth = turned[GROUP:], -turned[:GROUP]
    odd = jnp.concatenate([plain[:GROUP] + third, plain[GROUP:] - fourth], axis=0)
    last = jnp.concatenate([third, fourth], axis=0)
    return odd + (total + diff), last + (total - diff)


def name_channels(order_ref, group_ref, place_ref, high_ref, low_ref, names_ref):
    names_ref[...] = jnp.zeros_like(names_ref)
    names_ref[0, :SLOTS] = group_ref[...]
    names_ref[1, :SLOTS] = place_ref[...]
    blocks = high_ref.shape[0]
    width = blocks * BLOCK
    for row in range(0, blocks, 8):
        for col in range(0, width, GROUP):
            group = names_ref[0, row : row + 8, col : col + GROUP]
            place = names_ref[1, row : row + 8, col : col + GROUP]
            chan = jnp.zeros_like(place)
            for g in range(order_ref.shape[0]):
                names = jnp.broadcast_to(order_ref[g : g + 1, :], (8, GROUP))
                chan = jnp.where(group == g, lane_pick(names, place), chan)
            names_ref[0, row : row + 8, col : col + GROUP] = chan
    chan = names_ref[0]
    slot = lax.broadcasted_iota(jnp.int32, (blocks, LANES), 0)
    lane = lax.broadcasted_iota(jnp.int32, (blocks, LANES), 1)
    repeat = jnp.where(lax.shift_right_logical(lane, 3) == slot, 1.0, 0.0).astype(BF16)
    row = lax.broadcasted_iota(jnp.int32, (width, LANES), 0)
    lane = lax.broadcasted_iota(jnp.int32, (width, LANES), 1)
    own = jnp.bitwise_and(row, BLOCK - 1) == jnp.bitwise_and(lane, BLOCK - 1)
    for out_ref, part in (
        (high_ref, lax.shift_right_logical(chan, 8)),
        (low_ref, jnp.bitwise_and(chan, LANES - 1)),
    ):
        turned = part.astype(F32).T.astype(BF16)
        wide = jnp.dot(turned, repeat, preferred_element_type=F32)
        wide = jnp.where(own, wide, 0.0).reshape(blocks, BLOCK, LANES)
        out_ref[...] = jnp.sum(wide, axis=1).astype(jnp.int32)


def template_kernel(
    waves_ref, order_ref, group_ref, place_ref, table_ref, spec_ref, high_ref, low_ref, pad_ref, names_ref
):
    name_channels(order_ref, group_ref, place_ref, high_ref, low_ref, names_ref)
    pad_ref[...] = jnp.zeros_like(pad_ref)
    pad_ref[:USED, :TAPS] = waves_ref[...]
    waves = pad_ref[...].T
    mean = jnp.sum(waves * waves, axis=0, keepdims=True) * (1.0 / TAPS)
    scale = 1.0 / (jnp.sqrt(mean + 1e-6) * np.float32(np.sqrt(TAPS * SLOTS)))
    waves = waves * scale
    pieces = [waves[at : at + QUARTER] for at in range(0, 4 * QUARTER, QUARTER)]
    total, *rest = transform(pieces, table_ref)
    for part, spec in enumerate(rest):
        spec_ref[part * QUARTER : (part + 1) * QUARTER] = spec
    real, imag = total[:GROUP], total[GROUP:]
    first = lax.broadcasted_iota(jnp.int32, real.shape, 0) == 0
    at = 3 * QUARTER
    spec_ref[at : at + GROUP] = real
    spec_ref[at + GROUP : at + 2 * GROUP] = jnp.where(first, 0.0, imag)
    spec_ref[at + 2 * GROUP :] = jnp.where(first, imag, real)


def lane_pick(source, index):
    return jnp.take_along_axis(source, index, axis=1)


def select_kernel(record_ref, high_ref, low_ref, out_ref):
    blocks = high_ref.shape[0]
    span, channels = record_ref.shape
    width = LANES
    parts = []
    for at in range(0, channels, width):
        parts.extend(split(record_ref[:, at : at + width]))
    parts = jnp.concatenate(parts, axis=0)
    row = lax.broadcasted_iota(jnp.int32, (width, LANES), 0)
    for block in range(blocks):
        high = high_ref[block : block + 1, :]
        hot = jnp.where(row == low_ref[block : block + 1, :], 1.0, 0.0).astype(BF16)
        both = jnp.dot(parts, hot, preferred_element_type=F32)
        picked = jnp.zeros((span, LANES), F32)
        for g in range(channels // width):
            at = 2 * span * g
            quarter = both[at : at + span] + both[at + span : at + 2 * span]
            picked = jnp.where(high == g, quarter, picked)
        out_ref[block] = picked


def route(block, plane):
    low, core, z = block // 16, block // 8 % 2, block % 8
    key = z ^ (4 * core)
    return (plane ^ key) * 4 + (low ^ (key & 1)) * 2 + core


def load_rows(recv_ref, plane, x_ref, first, count, at):
    span = recv_ref.shape[1]
    row = first
    while row < first + count:
        block, low = divmod(row, span)
        take = min(span - low, first + count - row)
        x_ref[at : at + take, :] = recv_ref[route(block, plane), low : low + take, :]
        row += take
        at += take


def ends_kernel(plane_ref, recv_ref, head_ref, tail_ref):
    plane = plane_ref[0]
    total = recv_ref.shape[0] * recv_ref.shape[1]
    load_rows(recv_ref, plane, head_ref, 0, NEXT, 0)
    load_rows(recv_ref, plane, tail_ref, total - BACK, BACK, 0)


def window_scale(x_ref, sq_ref, lags):
    rows = lags + TAPS
    sq = x_ref[:rows] * x_ref[:rows]
    for step in (1, 2, 4):
        sq_ref[:rows] = sq
        sq_ref[rows : rows + 8] = jnp.zeros((8, LANES), F32)
        sq = sq_ref[:rows] + sq_ref[step : rows + step]
    total = sq[74 * 8 : 74 * 8 + lags]
    length = 1
    have = rows
    at = {64: 0, 8: 64, 2: 72}
    while length < 64:
        have = have - 8 * length
        sq = sq[:have] + sq[8 * length : 8 * length + have]
        length *= 2
        if length in at:
            total = total + sq[8 * at[length] : 8 * at[length] + lags]
    return lax.rsqrt(total * (1.0 / TAPS) + 1e-6)


def segments(x_ref, sq_ref, spans, spec_ref, forward_ref, back_ref):
    scale = window_scale(x_ref, sq_ref, sum(spans))
    stacks = []
    base = 0
    for lags in spans:
        pieces = [x_ref[at : at + QUARTER] for at in range(base, base + 4 * QUARTER, QUARTER)]
        spectra = transform(pieces, forward_ref)
        parts = []
        for part, spectrum in enumerate(spectra):
            real, imag = spectrum[:GROUP], spectrum[GROUP:]
            at = (part - 1) % 4 * QUARTER
            wave_real, wave_imag = spec_ref[at : at + GROUP], spec_ref[at + GROUP : at + QUARTER]
            wave_last = wave_real if part else spec_ref[at + QUARTER : at + QUARTER + GROUP]
            product = [real * wave_real + imag * wave_imag, imag * wave_last - real * wave_imag]
            parts.append(dot3(back_ref, part, jnp.concatenate(product, axis=0)))
        first, second = combine(parts)
        corr = jnp.concatenate([first, second[: lags - QUARTER]], axis=0)
        corr = corr * scale[base : base + lags]
        folded = (corr[:, :GROUP] + corr[:, GROUP:]).T
        acc = folded[:BLOCK]
        for s in range(1, GROUP // BLOCK):
            acc = acc + folded[s * BLOCK : (s + 1) * BLOCK]
        stacks.append(acc)
        base += lags
    return stacks


def near_kernel(plane_ref, recv_ref, *refs):
    *refs, out_ref, x_ref, sq_ref = refs
    load_rows(recv_ref, plane_ref[0], x_ref, KEEP, HOP + 2 * HALF, 0)
    one, two = segments(x_ref, sq_ref, (HOP, HOP), *refs)
    out_ref[:, :HOP] = one
    out_ref[:, HOP:] = two


def back_kernel(plane_ref, recv_ref, tail_ref, *refs):
    *refs, send_ref, keep_ref, x_ref, sq_ref = refs
    x_ref[:BACK] = tail_ref[...]
    load_rows(recv_ref, plane_ref[0], x_ref, 0, 2 * HALF - BACK, BACK)
    (stack,) = segments(x_ref, sq_ref, (BACK + KEEP,), *refs)
    send_ref[...] = stack[:, :BACK]
    keep_ref[...] = stack[:, BACK:]


def last_kernel(plane_ref, recv_ref, head_ref, *refs):
    *refs, out_ref, x_ref, sq_ref = refs
    own = recv_ref.shape[0] * recv_ref.shape[1] - KEEP - 2 * HOP
    load_rows(recv_ref, plane_ref[0], x_ref, KEEP + 2 * HOP, own, 0)
    x_ref[own : own + NEXT] = head_ref[...]
    x_ref[own + NEXT : 2 * HALF] = jnp.zeros((2 * HALF - own - NEXT, LANES), F32)
    (out_ref[...],) = segments(x_ref, sq_ref, (MOST,), *refs)


def join_kernel(*refs):
    *parts, out_ref = refs
    at = 0
    for part in parts:
        out_ref[:, at : at + part.shape[1]] = part[...]
        at += part.shape[1]


def call(kernel, out_shape, scratch, flops, nbytes, mib, name, scalars=0):
    def run(*operands):
        smem = pl.BlockSpec(memory_space=pltpu.SMEM)
        vmem = pl.BlockSpec(memory_space=pltpu.VMEM)
        return pl.pallas_call(
            kernel,
            out_shape=out_shape,
            in_specs=[smem if i < scalars else vmem for i in range(len(operands))],
            scratch_shapes=scratch,
            compiler_params=pltpu.CompilerParams(vmem_limit_bytes=mib << 20),
            cost_estimate=pl.CostEstimate(flops=flops, bytes_accessed=nbytes, transcendentals=0),
            name=name,
        )(*operands)

    return run


def shards(record, channel_order, templates, group_of_slot, place_of_slot):
    blocks = lax.axis_size("tmpl")
    planes = lax.axis_size("chan")
    span = record.shape[1]
    lags = blocks * span
    forward, back = (jnp.asarray(t) for t in tables())
    across, along = [], []
    per_plane = blocks // planes
    for b in range(blocks):
        for z in range(planes):
            plane, lane = divmod(b, per_plane)
            keeper = route(lane * planes + z, plane)
            across.append((b * planes + z, keeper * planes + z))
            along.append((keeper * planes + z, keeper * planes + plane))
    raw = lax.ppermute(record.T, ("tmpl", "chan"), across)
    plane = lax.axis_index("chan").astype(jnp.int32).reshape(1)

    waves = templates.transpose(1, 0, 2).reshape(USED, TAPS)
    names = jax.ShapeDtypeStruct((blocks, LANES), jnp.int32)
    specs, high, low = call(
        template_kernel,
        (jax.ShapeDtypeStruct((3 * QUARTER + 3 * GROUP, LANES), F32), names, names),
        [
            pltpu.VMEM((LANES, 4 * QUARTER), F32),
            pltpu.VMEM((2, blocks, blocks * BLOCK), jnp.int32),
        ],
        2 * 3 * 4 * QUARTER * QUARTER * LANES,
        4 << 20,
        16,
        "template_spectra",
    )(
        waves,
        channel_order.reshape(-1, GROUP),
        group_of_slot.reshape(-1, SLOTS).T,
        place_of_slot.T,
        forward,
    )
    raw, high, low, plane, specs = lax.optimization_barrier((raw, high, low, plane, specs))
    raw = lax.ppermute(raw, ("tmpl", "chan"), along)
    sent = call(
        select_kernel,
        jax.ShapeDtypeStruct((blocks, span, LANES), F32),
        [],
        1 << 20,
        4 << 20,
        8,
        "select_channels",
    )(raw, high, low)
    recv = lax.all_to_all(sent, "tmpl", split_axis=0, concat_axis=0, tiled=True)
    rows = jax.ShapeDtypeStruct((BACK, LANES), F32), jax.ShapeDtypeStruct((NEXT, LANES), F32)
    head, tail = call(ends_kernel, rows[::-1], [], 0, 1 << 20, 8, "ends", 1)(plane, recv)
    up = [(z, (z + 1) % planes) for z in range(planes)]
    down = [(t, s) for s, t in up]
    after = lax.ppermute(head, "chan", down)
    before = lax.ppermute(tail, "chan", up)
    flops = 2 * 3 * (2 * HALF * HALF + HOP * 2 * HALF) * LANES
    shared = (specs, forward, back)

    def part(kernel, count, name, *lags):
        lines = pltpu.VMEM(((count - 1) * HOP + 2 * HALF + 8, LANES), F32)
        shape = tuple(jax.ShapeDtypeStruct((BLOCK, n), F32) for n in lags)
        return call(kernel, shape, [lines, lines], count * flops, 8 << 20, 24, name, 1)

    (middle,) = part(near_kernel, 2, "near_segments", 2 * HOP)(plane, recv, *shared)
    early, keep = part(back_kernel, 1, "back_segment", BACK, KEEP)(plane, recv, before, *shared)
    given = lax.ppermute(early, "chan", down)
    (last,) = part(last_kernel, 1, "last_segment", MOST)(plane, recv, after, *shared)
    joined = jax.ShapeDtypeStruct((BLOCK, blocks * span), F32)
    return call(join_kernel, joined, [], 0, 1 << 17, 8, "join")(keep, middle, last, given)


def solution(mesh):
    placed = (P(None, ("tmpl", "chan")), P(), P("tmpl", None, None), P(), P())
    return jax.shard_map(
        shards, mesh=mesh, in_specs=placed, out_specs=P("tmpl", "chan"), check_vma=False
    )
```

```python
import jax
import jax.numpy as jnp
import ml_dtypes
import numpy as np
from jax import lax
from jax.experimental import pallas as pl
from jax.experimental.pallas import tpu as pltpu
from jax.sharding import PartitionSpec as P

SLOTS = 30
TAPS = 600
BLOCK = 8
LANES = 256
USED = SLOTS * BLOCK
HALF = 512
HOP = 384
MOST = 408
GROUP = 128
QUARTER = 256
ROOT = float(np.sqrt(2.0))
BACK = 232
KEEP = 128
NEXT = 368

F32 = jnp.float32
BF16 = jnp.bfloat16


def split_np(table):
    hi = table.astype(ml_dtypes.bfloat16)
    lo = (table - hi.astype(np.float64)).astype(ml_dtypes.bfloat16)
    return hi, lo


def tables():
    n = np.arange(QUARTER, dtype=np.int64)[None, :]
    m = np.arange(GROUP, dtype=np.int64)[:, None]
    forward, back = [], []
    for eighths in (0, 4, 1, 3):
        if eighths in (0, 4):
            angle = ((2 * m + eighths // 4) * n % (2 * QUARTER)) * (np.pi / QUARTER)
            imag = -np.sin(angle)
            weight = np.full((QUARTER, 1), 2.0 / QUARTER)
            if not eighths:
                imag[0] = 1.0 - 2.0 * (n[0] % 2)
                weight[0] = weight[GROUP] = 1.0 / QUARTER
            table = np.concatenate([np.cos(angle), imag])
            inverse = (weight * table).T
        else:
            angle = ((8 * m + eighths) * n % (8 * GROUP)) * (np.pi / (4 * GROUP))
            table = np.concatenate([np.cos(angle), -np.sin(angle)])
            sign = 1.0 if eighths == 1 else -1.0
            cos, sin = np.cos(angle[:, :GROUP]).T / GROUP, np.sin(angle[:, :GROUP]).T / GROUP
            root = np.sqrt(2.0)
            low = np.concatenate([cos + sign * sin, sign * cos - sin], axis=1)
            high = np.concatenate([-root * sin, -root * cos], axis=1)
            inverse = np.concatenate([low, high])
        forward.append(table)
        back.append(0.25 * inverse)
    out = []
    for stack in (forward, back):
        hi, lo = split_np(np.concatenate(stack))
        out.append(np.concatenate([hi, hi, lo], axis=1))
    return out


def split(value):
    hi = value.astype(BF16)
    lo = (value - hi.astype(F32)).astype(BF16)
    return hi, lo


def dot3(table_ref, part, value):
    hi, lo = split(value)
    both = jnp.concatenate([hi, lo, hi], axis=0)
    rows = table_ref[part * QUARTER : (part + 1) * QUARTER]
    return jnp.dot(rows, both, preferred_element_type=F32)


def transform(pieces, table_ref):
    one, two, three, four = pieces
    even, late = one + three, two + four
    odd, last = one - three, two - four
    third, fourth = last[:GROUP], last[GROUP:]
    plain = jnp.concatenate([odd[:GROUP] - third, odd[GROUP:] + fourth], axis=0)
    turned = ROOT * jnp.concatenate([fourth, -third], axis=0)
    residues = (even + late, even - late, plain - turned, plain + turned)
    return [dot3(table_ref, part, value) for part, value in enumerate(residues)]


def combine(parts):
    total, diff, left, right = parts
    plain = left + right
    turned = (left - right) * (1.0 / ROOT)
    third, fourth = turned[GROUP:], -turned[:GROUP]
    odd = jnp.concatenate([plain[:GROUP] + third, plain[GROUP:] - fourth], axis=0)
    last = jnp.concatenate([third, fourth], axis=0)
    return odd + (total + diff), last + (total - diff)


def name_channels(order_ref, group_ref, place_ref, high_ref, low_ref, names_ref):
    names_ref[...] = jnp.zeros_like(names_ref)
    names_ref[0, :SLOTS] = group_ref[...]
    names_ref[1, :SLOTS] = place_ref[...]
    blocks = high_ref.shape[0]
    width = blocks * BLOCK
    for row in range(0, blocks, 8):
        for col in range(0, width, GROUP):
            group = names_ref[0, row : row + 8, col : col + GROUP]
            place = names_ref[1, row : row + 8, col : col + GROUP]
            chan = jnp.zeros_like(place)
            for g in range(order_ref.shape[0]):
                names = jnp.broadcast_to(order_ref[g : g + 1, :], (8, GROUP))
                chan = jnp.where(group == g, lane_pick(names, place), chan)
            names_ref[0, row : row + 8, col : col + GROUP] = chan
    chan = names_ref[0]
    slot = lax.broadcasted_iota(jnp.int32, (blocks, LANES), 0)
    lane = lax.broadcasted_iota(jnp.int32, (blocks, LANES), 1)
    repeat = jnp.where(lax.shift_right_logical(lane, 3) == slot, 1.0, 0.0).astype(BF16)
    row = lax.broadcasted_iota(jnp.int32, (width, LANES), 0)
    lane = lax.broadcasted_iota(jnp.int32, (width, LANES), 1)
    own = jnp.bitwise_and(row, BLOCK - 1) == jnp.bitwise_and(lane, BLOCK - 1)
    for out_ref, part in (
        (high_ref, lax.shift_right_logical(chan, 8)),
        (low_ref, jnp.bitwise_and(chan, LANES - 1)),
    ):
        turned = part.astype(F32).T.astype(BF16)
        wide = jnp.dot(turned, repeat, preferred_element_type=F32)
        wide = jnp.where(own, wide, 0.0).reshape(blocks, BLOCK, LANES)
        out_ref[...] = jnp.sum(wide, axis=1).astype(jnp.int32)


def template_kernel(
    waves_ref, order_ref, group_ref, place_ref, table_ref, spec_ref, high_ref, low_ref, pad_ref, names_ref
):
    name_channels(order_ref, group_ref, place_ref, high_ref, low_ref, names_ref)
    pad_ref[...] = jnp.zeros_like(pad_ref)
    pad_ref[:USED, :TAPS] = waves_ref[...]
    waves = pad_ref[...].T
    mean = jnp.sum(waves * waves, axis=0, keepdims=True) * (1.0 / TAPS)
    scale = 1.0 / (jnp.sqrt(mean + 1e-6) * np.float32(np.sqrt(TAPS * SLOTS)))
    waves = waves * scale
    pieces = [waves[at : at + QUARTER] for at in range(0, 4 * QUARTER, QUARTER)]
    total, *rest = transform(pieces, table_ref)
    for part, spec in enumerate(rest):
        spec_ref[part * QUARTER : (part + 1) * QUARTER] = spec
    real, imag = total[:GROUP], total[GROUP:]
    first = lax.broadcasted_iota(jnp.int32, real.shape, 0) == 0
    at = 3 * QUARTER
    spec_ref[at : at + GROUP] = real
    spec_ref[at + GROUP : at + 2 * GROUP] = jnp.where(first, 0.0, imag)
    spec_ref[at + 2 * GROUP :] = jnp.where(first, imag, real)


def lane_pick(source, index):
    return jnp.take_along_axis(source, index, axis=1)


def select_kernel(record_ref, high_ref, low_ref, out_ref):
    blocks = high_ref.shape[0]
    span, channels = record_ref.shape
    width = LANES
    parts = []
    for at in range(0, channels, width):
        parts.extend(split(record_ref[:, at : at + width]))
    parts = jnp.concatenate(parts, axis=0)
    row = lax.broadcasted_iota(jnp.int32, (width, LANES), 0)
    for block in range(blocks):
        high = high_ref[block : block + 1, :]
        hot = jnp.where(row == low_ref[block : block + 1, :], 1.0, 0.0).astype(BF16)
        both = jnp.dot(parts, hot, preferred_element_type=F32)
        picked = jnp.zeros((span, LANES), F32)
        for g in range(channels // width):
            at = 2 * span * g
            quarter = both[at : at + span] + both[at + span : at + 2 * span]
            picked = jnp.where(high == g, quarter, picked)
        out_ref[block] = picked


def route(block, plane):
    low, core, z = block // 16, block // 8 % 2, block % 8
    far = plane ^ z
    key = (far & 1) * 7 ^ (far >> 1 & 1) * 5 ^ (far >> 2 & 1) ^ (3 * core)
    return (plane ^ key) * 4 + (low ^ (key & 1)) * 2 + core


def load_rows(recv_ref, plane, x_ref, first, count, at):
    span = recv_ref.shape[1]
    row = first
    while row < first + count:
        block, low = divmod(row, span)
        take = min(span - low, first + count - row)
        x_ref[at : at + take, :] = recv_ref[route(block, plane), low : low + take, :]
        row += take
        at += take


def ends_kernel(plane_ref, recv_ref, head_ref, tail_ref):
    plane = plane_ref[0]
    total = recv_ref.shape[0] * recv_ref.shape[1]
    load_rows(recv_ref, plane, head_ref, 0, NEXT, 0)
    load_rows(recv_ref, plane, tail_ref, total - BACK, BACK, 0)


def window_scale(x_ref, sq_ref, lags):
    rows = lags + TAPS
    sq = x_ref[:rows] * x_ref[:rows]
    for step in (1, 2, 4):
        sq_ref[:rows] = sq
        sq_ref[rows : rows + 8] = jnp.zeros((8, LANES), F32)
        sq = sq_ref[:rows] + sq_ref[step : rows + step]
    total = sq[74 * 8 : 74 * 8 + lags]
    length = 1
    have = rows
    at = {64: 0, 8: 64, 2: 72}
    while length < 64:
        have = have - 8 * length
        sq = sq[:have] + sq[8 * length : 8 * length + have]
        length *= 2
        if length in at:
            total = total + sq[8 * at[length] : 8 * at[length] + lags]
    return lax.rsqrt(total * (1.0 / TAPS) + 1e-6)


def segments(x_ref, sq_ref, spans, spec_ref, forward_ref, back_ref):
    scale = window_scale(x_ref, sq_ref, sum(spans))
    stacks = []
    base = 0
    for lags in spans:
        pieces = [x_ref[at : at + QUARTER] for at in range(base, base + 4 * QUARTER, QUARTER)]
        spectra = transform(pieces, forward_ref)
        parts = []
        for part, spectrum in enumerate(spectra):
            real, imag = spectrum[:GROUP], spectrum[GROUP:]
            at = (part - 1) % 4 * QUARTER
            wave_real, wave_imag = spec_ref[at : at + GROUP], spec_ref[at + GROUP : at + QUARTER]
            wave_last = wave_real if part else spec_ref[at + QUARTER : at + QUARTER + GROUP]
            product = [real * wave_real + imag * wave_imag, imag * wave_last - real * wave_imag]
            parts.append(dot3(back_ref, part, jnp.concatenate(product, axis=0)))
        first, second = combine(parts)
        corr = jnp.concatenate([first, second[: lags - QUARTER]], axis=0)
        corr = corr * scale[base : base + lags]
        folded = (corr[:, :GROUP] + corr[:, GROUP:]).T
        acc = folded[:BLOCK]
        for s in range(1, GROUP // BLOCK):
            acc = acc + folded[s * BLOCK : (s + 1) * BLOCK]
        stacks.append(acc)
        base += lags
    return stacks


def near_kernel(plane_ref, recv_ref, *refs):
    *refs, out_ref, x_ref, sq_ref = refs
    load_rows(recv_ref, plane_ref[0], x_ref, KEEP, HOP + 2 * HALF, 0)
    one, two = segments(x_ref, sq_ref, (HOP, HOP), *refs)
    out_ref[:, :HOP] = one
    out_ref[:, HOP:] = two


def back_kernel(plane_ref, recv_ref, tail_ref, *refs):
    *refs, send_ref, keep_ref, x_ref, sq_ref = refs
    x_ref[:BACK] = tail_ref[...]
    load_rows(recv_ref, plane_ref[0], x_ref, 0, 2 * HALF - BACK, BACK)
    (stack,) = segments(x_ref, sq_ref, (BACK + KEEP,), *refs)
    send_ref[...] = stack[:, :BACK]
    keep_ref[...] = stack[:, BACK:]


def last_kernel(plane_ref, recv_ref, head_ref, *refs):
    *refs, out_ref, x_ref, sq_ref = refs
    own = recv_ref.shape[0] * recv_ref.shape[1] - KEEP - 2 * HOP
    load_rows(recv_ref, plane_ref[0], x_ref, KEEP + 2 * HOP, own, 0)
    x_ref[own : own + NEXT] = head_ref[...]
    x_ref[own + NEXT : 2 * HALF] = jnp.zeros((2 * HALF - own - NEXT, LANES), F32)
    (out_ref[...],) = segments(x_ref, sq_ref, (MOST,), *refs)


def join_kernel(*refs):
    *parts, out_ref = refs
    at = 0
    for part in parts:
        out_ref[:, at : at + part.shape[1]] = part[...]
        at += part.shape[1]


def call(kernel, out_shape, scratch, flops, nbytes, mib, name, scalars=0):
    def run(*operands):
        smem = pl.BlockSpec(memory_space=pltpu.SMEM)
        vmem = pl.BlockSpec(memory_space=pltpu.VMEM)
        return pl.pallas_call(
            kernel,
            out_shape=out_shape,
            in_specs=[smem if i < scalars else vmem for i in range(len(operands))],
            scratch_shapes=scratch,
            compiler_params=pltpu.CompilerParams(vmem_limit_bytes=mib << 20),
            cost_estimate=pl.CostEstimate(flops=flops, bytes_accessed=nbytes, transcendentals=0),
            name=name,
        )(*operands)

    return run


def shards(record, channel_order, templates, group_of_slot, place_of_slot):
    blocks = lax.axis_size("tmpl")
    planes = lax.axis_size("chan")
    span = record.shape[1]
    lags = blocks * span
    forward, back = (jnp.asarray(t) for t in tables())
    across, along = [], []
    per_plane = blocks // planes
    for b in range(blocks):
        for z in range(planes):
            plane, lane = divmod(b, per_plane)
            keeper = route(lane * planes + z, plane)
            across.append((b * planes + z, keeper * planes + z))
            along.append((keeper * planes + z, keeper * planes + plane))
    raw = lax.ppermute(record.T, ("tmpl", "chan"), across)
    plane = lax.axis_index("chan").astype(jnp.int32).reshape(1)

    waves = templates.transpose(1, 0, 2).reshape(USED, TAPS)
    names = jax.ShapeDtypeStruct((blocks, LANES), jnp.int32)
    specs, high, low = call(
        template_kernel,
        (jax.ShapeDtypeStruct((3 * QUARTER + 3 * GROUP, LANES), F32), names, names),
        [
            pltpu.VMEM((LANES, 4 * QUARTER), F32),
            pltpu.VMEM((2, blocks, blocks * BLOCK), jnp.int32),
        ],
        2 * 3 * 4 * QUARTER * QUARTER * LANES,
        4 << 20,
        16,
        "template_spectra",
    )(
        waves,
        channel_order.reshape(-1, GROUP),
        group_of_slot.reshape(-1, SLOTS).T,
        place_of_slot.T,
        forward,
    )
    raw, high, low, plane, specs = lax.optimization_barrier((raw, high, low, plane, specs))
    raw = lax.ppermute(raw, ("tmpl", "chan"), along)
    sent = call(
        select_kernel,
        jax.ShapeDtypeStruct((blocks, span, LANES), F32),
        [],
        1 << 20,
        4 << 20,
        8,
        "select_channels",
    )(raw, high, low)
    recv = lax.all_to_all(sent, "tmpl", split_axis=0, concat_axis=0, tiled=True)
    rows = jax.ShapeDtypeStruct((BACK, LANES), F32), jax.ShapeDtypeStruct((NEXT, LANES), F32)
    head, tail = call(ends_kernel, rows[::-1], [], 0, 1 << 20, 8, "ends", 1)(plane, recv)
    up = [(z, (z + 1) % planes) for z in range(planes)]
    down = [(t, s) for s, t in up]
    after = lax.ppermute(head, "chan", down)
    before = lax.ppermute(tail, "chan", up)
    flops = 2 * 3 * (2 * HALF * HALF + HOP * 2 * HALF) * LANES
    shared = (specs, forward, back)

    def part(kernel, count, name, *lags):
        lines = pltpu.VMEM(((count - 1) * HOP + 2 * HALF + 8, LANES), F32)
        shape = tuple(jax.ShapeDtypeStruct((BLOCK, n), F32) for n in lags)
        return call(kernel, shape, [lines, lines], count * flops, 8 << 20, 24, name, 1)

    (middle,) = part(near_kernel, 2, "near_segments", 2 * HOP)(plane, recv, *shared)
    early, keep = part(back_kernel, 1, "back_segment", BACK, KEEP)(plane, recv, before, *shared)
    given = lax.ppermute(early, "chan", down)
    (last,) = part(last_kernel, 1, "last_segment", MOST)(plane, recv, after, *shared)
    joined = jax.ShapeDtypeStruct((BLOCK, blocks * span), F32)
    return call(join_kernel, joined, [], 0, 1 << 17, 8, "join")(keep, middle, last, given)


def solution(mesh):
    placed = (P(None, ("tmpl", "chan")), P(), P("tmpl", None, None), P(), P())
    return jax.shard_map(
        shards, mesh=mesh, in_specs=placed, out_specs=P("tmpl", "chan"), check_vma=False
    )
```

```python
import jax
import jax.numpy as jnp
import ml_dtypes
import numpy as np
from jax import lax
from jax.experimental import pallas as pl
from jax.experimental.pallas import tpu as pltpu
from jax.sharding import PartitionSpec as P

SLOTS = 30
TAPS = 600
BLOCK = 8
LANES = 256
USED = SLOTS * BLOCK
HALF = 512
HOP = 384
MOST = 408
GROUP = 128
QUARTER = 256
ROOT = float(np.sqrt(2.0))
BACK = 232
KEEP = 128
NEXT = 368

F32 = jnp.float32
BF16 = jnp.bfloat16


def split_np(table):
    hi = table.astype(ml_dtypes.bfloat16)
    lo = (table - hi.astype(np.float64)).astype(ml_dtypes.bfloat16)
    return hi, lo


def tables():
    n = np.arange(QUARTER, dtype=np.int64)[None, :]
    m = np.arange(GROUP, dtype=np.int64)[:, None]
    forward, back = [], []
    for eighths in (0, 4, 1, 3):
        if eighths in (0, 4):
            angle = ((2 * m + eighths // 4) * n % (2 * QUARTER)) * (np.pi / QUARTER)
            imag = -np.sin(angle)
            weight = np.full((QUARTER, 1), 2.0 / QUARTER)
            if not eighths:
                imag[0] = 1.0 - 2.0 * (n[0] % 2)
                weight[0] = weight[GROUP] = 1.0 / QUARTER
            table = np.concatenate([np.cos(angle), imag])
            inverse = (weight * table).T
        else:
            angle = ((8 * m + eighths) * n % (8 * GROUP)) * (np.pi / (4 * GROUP))
            table = np.concatenate([np.cos(angle), -np.sin(angle)])
            sign = 1.0 if eighths == 1 else -1.0
            cos, sin = np.cos(angle[:, :GROUP]).T / GROUP, np.sin(angle[:, :GROUP]).T / GROUP
            root = np.sqrt(2.0)
            low = np.concatenate([cos + sign * sin, sign * cos - sin], axis=1)
            high = np.concatenate([-root * sin, -root * cos], axis=1)
            inverse = np.concatenate([low, high])
        forward.append(table)
        back.append(0.25 * inverse)
    out = []
    for stack in (forward, back):
        hi, lo = split_np(np.concatenate(stack))
        out.append(np.concatenate([hi, hi, lo], axis=1))
    return out


def split(value):
    hi = value.astype(BF16)
    lo = (value - hi.astype(F32)).astype(BF16)
    return hi, lo


def dot3(table_ref, part, value):
    hi, lo = split(value)
    both = jnp.concatenate([hi, lo, hi], axis=0)
    rows = table_ref[part * QUARTER : (part + 1) * QUARTER]
    return jnp.dot(rows, both, preferred_element_type=F32)


def transform(pieces, table_ref):
    one, two, three, four = pieces
    even, late = one + three, two + four
    odd, last = one - three, two - four
    third, fourth = last[:GROUP], last[GROUP:]
    plain = jnp.concatenate([odd[:GROUP] - third, odd[GROUP:] + fourth], axis=0)
    turned = ROOT * jnp.concatenate([fourth, -third], axis=0)
    residues = (even + late, even - late, plain - turned, plain + turned)
    return [dot3(table_ref, part, value) for part, value in enumerate(residues)]


def combine(parts):
    total, diff, left, right = parts
    plain = left + right
    turned = (left - right) * (1.0 / ROOT)
    third, fourth = turned[GROUP:], -turned[:GROUP]
    odd = jnp.concatenate([plain[:GROUP] + third, plain[GROUP:] - fourth], axis=0)
    last = jnp.concatenate([third, fourth], axis=0)
    return odd + (total + diff), last + (total - diff)


def name_channels(order_ref, group_ref, place_ref, high_ref, low_ref, names_ref):
    names_ref[...] = jnp.zeros_like(names_ref)
    names_ref[0, :SLOTS] = group_ref[...]
    names_ref[1, :SLOTS] = place_ref[...]
    blocks = high_ref.shape[0]
    width = blocks * BLOCK
    for row in range(0, blocks, 8):
        for col in range(0, width, GROUP):
            group = names_ref[0, row : row + 8, col : col + GROUP]
            place = names_ref[1, row : row + 8, col : col + GROUP]
            chan = jnp.zeros_like(place)
            for g in range(order_ref.shape[0]):
                names = jnp.broadcast_to(order_ref[g : g + 1, :], (8, GROUP))
                chan = jnp.where(group == g, lane_pick(names, place), chan)
            names_ref[0, row : row + 8, col : col + GROUP] = chan
    chan = names_ref[0]
    slot = lax.broadcasted_iota(jnp.int32, (blocks, LANES), 0)
    lane = lax.broadcasted_iota(jnp.int32, (blocks, LANES), 1)
    repeat = jnp.where(lax.shift_right_logical(lane, 3) == slot, 1.0, 0.0).astype(BF16)
    row = lax.broadcasted_iota(jnp.int32, (width, LANES), 0)
    lane = lax.broadcasted_iota(jnp.int32, (width, LANES), 1)
    own = jnp.bitwise_and(row, BLOCK - 1) == jnp.bitwise_and(lane, BLOCK - 1)
    for out_ref, part in (
        (high_ref, lax.shift_right_logical(chan, 8)),
        (low_ref, jnp.bitwise_and(chan, LANES - 1)),
    ):
        turned = part.astype(F32).T.astype(BF16)
        wide = jnp.dot(turned, repeat, preferred_element_type=F32)
        wide = jnp.where(own, wide, 0.0).reshape(blocks, BLOCK, LANES)
        out_ref[...] = jnp.sum(wide, axis=1).astype(jnp.int32)


def template_kernel(
    waves_ref, order_ref, group_ref, place_ref, table_ref, spec_ref, high_ref, low_ref, pad_ref, names_ref
):
    name_channels(order_ref, group_ref, place_ref, high_ref, low_ref, names_ref)
    pad_ref[...] = jnp.zeros_like(pad_ref)
    pad_ref[:USED, :TAPS] = waves_ref[...]
    waves = pad_ref[...].T
    mean = jnp.sum(waves * waves, axis=0, keepdims=True) * (1.0 / TAPS)
    scale = 1.0 / (jnp.sqrt(mean + 1e-6) * np.float32(np.sqrt(TAPS * SLOTS)))
    waves = waves * scale
    pieces = [waves[at : at + QUARTER] for at in range(0, 4 * QUARTER, QUARTER)]
    total, *rest = transform(pieces, table_ref)
    for part, spec in enumerate(rest):
        spec_ref[part * QUARTER : (part + 1) * QUARTER] = spec
    real, imag = total[:GROUP], total[GROUP:]
    first = lax.broadcasted_iota(jnp.int32, real.shape, 0) == 0
    at = 3 * QUARTER
    spec_ref[at : at + GROUP] = real
    spec_ref[at + GROUP : at + 2 * GROUP] = jnp.where(first, 0.0, imag)
    spec_ref[at + 2 * GROUP :] = jnp.where(first, imag, real)


def lane_pick(source, index):
    return jnp.take_along_axis(source, index, axis=1)


def select_kernel(record_ref, high_ref, low_ref, out_ref):
    blocks = high_ref.shape[0]
    span, channels = record_ref.shape
    width = LANES
    parts = []
    for at in range(0, channels, width):
        parts.extend(split(record_ref[:, at : at + width]))
    parts = jnp.concatenate(parts, axis=0)
    row = lax.broadcasted_iota(jnp.int32, (width, LANES), 0).astype(F32).astype(BF16)
    one, zero = jnp.ones((), BF16), jnp.zeros((), BF16)
    for block in range(blocks):
        high = high_ref[block : block + 1, :]
        low = low_ref[block : block + 1, :].astype(F32).astype(BF16)
        hot = jnp.where(row == low, one, zero)
        both = jnp.dot(parts, hot, preferred_element_type=F32)
        picked = jnp.zeros((span, LANES), F32)
        for g in range(channels // width):
            at = 2 * span * g
            quarter = both[at : at + span] + both[at + span : at + 2 * span]
            picked = jnp.where(high == g, quarter, picked)
        out_ref[block] = picked


def route(block, plane):
    low, core, z = block // 16, block // 8 % 2, block % 8
    far = plane ^ z
    key = (far & 1) * 7 ^ (far >> 1 & 1) * 5 ^ (far >> 2 & 1) ^ (3 * core)
    return (plane ^ key) * 4 + (low ^ (key & 1)) * 2 + core


def load_rows(recv_ref, plane, x_ref, first, count, at):
    span = recv_ref.shape[1]
    row = first
    while row < first + count:
        block, low = divmod(row, span)
        take = min(span - low, first + count - row)
        x_ref[at : at + take, :] = recv_ref[route(block, plane), low : low + take, :]
        row += take
        at += take


def ends_kernel(plane_ref, recv_ref, head_ref, tail_ref):
    plane = plane_ref[0]
    total = recv_ref.shape[0] * recv_ref.shape[1]
    load_rows(recv_ref, plane, head_ref, 0, NEXT, 0)
    load_rows(recv_ref, plane, tail_ref, total - BACK, BACK, 0)


def window_scale(x_ref, sq_ref, lags):
    rows = lags + TAPS
    sq = x_ref[:rows] * x_ref[:rows]
    for step in (1, 2, 4):
        sq_ref[:rows] = sq
        sq_ref[rows : rows + 8] = jnp.zeros((8, LANES), F32)
        sq = sq_ref[:rows] + sq_ref[step : rows + step]
    total = sq[74 * 8 : 74 * 8 + lags]
    length = 1
    have = rows
    at = {64: 0, 8: 64, 2: 72}
    while length < 64:
        have = have - 8 * length
        sq = sq[:have] + sq[8 * length : 8 * length + have]
        length *= 2
        if length in at:
            total = total + sq[8 * at[length] : 8 * at[length] + lags]
    return lax.rsqrt(total * (1.0 / TAPS) + 1e-6)


def segments(x_ref, sq_ref, spans, spec_ref, forward_ref, back_ref):
    scale = window_scale(x_ref, sq_ref, sum(spans))
    stacks = []
    base = 0
    for lags in spans:
        pieces = [x_ref[at : at + QUARTER] for at in range(base, base + 4 * QUARTER, QUARTER)]
        spectra = transform(pieces, forward_ref)
        parts = []
        for part, spectrum in enumerate(spectra):
            real, imag = spectrum[:GROUP], spectrum[GROUP:]
            at = (part - 1) % 4 * QUARTER
            wave_real, wave_imag = spec_ref[at : at + GROUP], spec_ref[at + GROUP : at + QUARTER]
            wave_last = wave_real if part else spec_ref[at + QUARTER : at + QUARTER + GROUP]
            product = [real * wave_real + imag * wave_imag, imag * wave_last - real * wave_imag]
            parts.append(dot3(back_ref, part, jnp.concatenate(product, axis=0)))
        first, second = combine(parts)
        corr = jnp.concatenate([first, second[: lags - QUARTER]], axis=0)
        corr = corr * scale[base : base + lags]
        folded = (corr[:, :GROUP] + corr[:, GROUP:]).T
        acc = folded[:BLOCK]
        for s in range(1, GROUP // BLOCK):
            acc = acc + folded[s * BLOCK : (s + 1) * BLOCK]
        stacks.append(acc)
        base += lags
    return stacks


def near_kernel(plane_ref, recv_ref, *refs):
    *refs, out_ref, x_ref, sq_ref = refs
    load_rows(recv_ref, plane_ref[0], x_ref, KEEP, HOP + 2 * HALF, 0)
    one, two = segments(x_ref, sq_ref, (HOP, HOP), *refs)
    out_ref[:, :HOP] = one
    out_ref[:, HOP:] = two


def back_kernel(plane_ref, recv_ref, tail_ref, *refs):
    *refs, send_ref, keep_ref, x_ref, sq_ref = refs
    x_ref[:BACK] = tail_ref[...]
    load_rows(recv_ref, plane_ref[0], x_ref, 0, 2 * HALF - BACK, BACK)
    (stack,) = segments(x_ref, sq_ref, (BACK + KEEP,), *refs)
    send_ref[...] = stack[:, :BACK]
    keep_ref[...] = stack[:, BACK:]


def last_kernel(plane_ref, recv_ref, head_ref, *refs):
    *refs, out_ref, x_ref, sq_ref = refs
    own = recv_ref.shape[0] * recv_ref.shape[1] - KEEP - 2 * HOP
    load_rows(recv_ref, plane_ref[0], x_ref, KEEP + 2 * HOP, own, 0)
    x_ref[own : own + NEXT] = head_ref[...]
    x_ref[own + NEXT : 2 * HALF] = jnp.zeros((2 * HALF - own - NEXT, LANES), F32)
    (out_ref[...],) = segments(x_ref, sq_ref, (MOST,), *refs)


def join_kernel(*refs):
    *parts, out_ref = refs
    at = 0
    for part in parts:
        out_ref[:, at : at + part.shape[1]] = part[...]
        at += part.shape[1]


def call(kernel, out_shape, scratch, flops, nbytes, mib, name, scalars=0):
    def run(*operands):
        smem = pl.BlockSpec(memory_space=pltpu.SMEM)
        vmem = pl.BlockSpec(memory_space=pltpu.VMEM)
        return pl.pallas_call(
            kernel,
            out_shape=out_shape,
            in_specs=[smem if i < scalars else vmem for i in range(len(operands))],
            scratch_shapes=scratch,
            compiler_params=pltpu.CompilerParams(vmem_limit_bytes=mib << 20),
            cost_estimate=pl.CostEstimate(flops=flops, bytes_accessed=nbytes, transcendentals=0),
            name=name,
        )(*operands)

    return run


def shards(record, channel_order, templates, group_of_slot, place_of_slot):
    blocks = lax.axis_size("tmpl")
    planes = lax.axis_size("chan")
    span = record.shape[1]
    lags = blocks * span
    forward, back = (jnp.asarray(t) for t in tables())
    across, along = [], []
    per_plane = blocks // planes
    for b in range(blocks):
        for z in range(planes):
            plane, lane = divmod(b, per_plane)
            keeper = route(lane * planes + z, plane)
            across.append((b * planes + z, keeper * planes + z))
            along.append((keeper * planes + z, keeper * planes + plane))
    raw = lax.ppermute(record.T, ("tmpl", "chan"), across)
    plane = lax.axis_index("chan").astype(jnp.int32).reshape(1)

    waves = templates.transpose(1, 0, 2).reshape(USED, TAPS)
    small = (
        waves,
        channel_order.reshape(-1, GROUP),
        group_of_slot.reshape(-1, SLOTS).T,
        place_of_slot.T,
    )
    raw, plane, small = lax.optimization_barrier((raw, plane, small))
    raw = lax.ppermute(raw, ("tmpl", "chan"), along)
    names = jax.ShapeDtypeStruct((blocks, LANES), jnp.int32)
    specs, high, low = call(
        template_kernel,
        (jax.ShapeDtypeStruct((3 * QUARTER + 3 * GROUP, LANES), F32), names, names),
        [
            pltpu.VMEM((LANES, 4 * QUARTER), F32),
            pltpu.VMEM((2, blocks, blocks * BLOCK), jnp.int32),
        ],
        2 * 3 * 4 * QUARTER * QUARTER * LANES,
        4 << 20,
        16,
        "template_spectra",
    )(*small, forward)
    raw, high, low, specs = lax.optimization_barrier((raw, high, low, specs))
    sent = call(
        select_kernel,
        jax.ShapeDtypeStruct((blocks, span, LANES), F32),
        [],
        1 << 20,
        4 << 20,
        8,
        "select_channels",
    )(raw, high, low)
    recv = lax.all_to_all(sent, "tmpl", split_axis=0, concat_axis=0, tiled=True)
    rows = jax.ShapeDtypeStruct((BACK, LANES), F32), jax.ShapeDtypeStruct((NEXT, LANES), F32)
    head, tail = call(ends_kernel, rows[::-1], [], 0, 1 << 20, 8, "ends", 1)(plane, recv)
    up = [(z, (z + 1) % planes) for z in range(planes)]
    down = [(t, s) for s, t in up]
    after = lax.ppermute(head, "chan", down)
    before = lax.ppermute(tail, "chan", up)
    flops = 2 * 3 * (2 * HALF * HALF + HOP * 2 * HALF) * LANES
    shared = (specs, forward, back)

    def part(kernel, count, name, *lags):
        lines = pltpu.VMEM(((count - 1) * HOP + 2 * HALF + 8, LANES), F32)
        shape = tuple(jax.ShapeDtypeStruct((BLOCK, n), F32) for n in lags)
        return call(kernel, shape, [lines, lines], count * flops, 8 << 20, 24, name, 1)

    (middle,) = part(near_kernel, 2, "near_segments", 2 * HOP)(plane, recv, *shared)
    early, keep = part(back_kernel, 1, "back_segment", BACK, KEEP)(plane, recv, before, *shared)
    given = lax.ppermute(early, "chan", down)
    (last,) = part(last_kernel, 1, "last_segment", MOST)(plane, recv, after, *shared)
    joined = jax.ShapeDtypeStruct((BLOCK, blocks * span), F32)
    return call(join_kernel, joined, [], 0, 1 << 17, 8, "join")(keep, middle, last, given)


def solution(mesh):
    placed = (P(None, ("tmpl", "chan")), P(), P("tmpl", None, None), P(), P())
    return jax.shard_map(
        shards, mesh=mesh, in_specs=placed, out_specs=P("tmpl", "chan"), check_vma=False
    )
```

```python
import jax
import jax.numpy as jnp
import ml_dtypes
import numpy as np
from jax import lax
from jax.experimental import pallas as pl
from jax.experimental.pallas import tpu as pltpu
from jax.sharding import PartitionSpec as P

SLOTS = 30
TAPS = 600
BLOCK = 8
LANES = 256
USED = SLOTS * BLOCK
HALF = 512
HOP = 384
MOST = 408
GROUP = 128
QUARTER = 256
ROOT = float(np.sqrt(2.0))
BACK = 232
KEEP = 128
NEXT = 368

F32 = jnp.float32
BF16 = jnp.bfloat16


def split_np(table):
    hi = table.astype(ml_dtypes.bfloat16)
    lo = (table - hi.astype(np.float64)).astype(ml_dtypes.bfloat16)
    return hi, lo


def tables():
    n = np.arange(QUARTER, dtype=np.int64)[None, :]
    m = np.arange(GROUP, dtype=np.int64)[:, None]
    forward, back = [], []
    for eighths in (0, 4, 1, 3):
        if eighths in (0, 4):
            angle = ((2 * m + eighths // 4) * n % (2 * QUARTER)) * (np.pi / QUARTER)
            imag = -np.sin(angle)
            weight = np.full((QUARTER, 1), 2.0 / QUARTER)
            if not eighths:
                imag[0] = 1.0 - 2.0 * (n[0] % 2)
                weight[0] = weight[GROUP] = 1.0 / QUARTER
            table = np.concatenate([np.cos(angle), imag])
            inverse = (weight * table).T
        else:
            angle = ((8 * m + eighths) * n % (8 * GROUP)) * (np.pi / (4 * GROUP))
            table = np.concatenate([np.cos(angle), -np.sin(angle)])
            sign = 1.0 if eighths == 1 else -1.0
            cos, sin = np.cos(angle[:, :GROUP]).T / GROUP, np.sin(angle[:, :GROUP]).T / GROUP
            root = np.sqrt(2.0)
            low = np.concatenate([cos + sign * sin, sign * cos - sin], axis=1)
            high = np.concatenate([-root * sin, -root * cos], axis=1)
            inverse = np.concatenate([low, high])
        forward.append(table)
        back.append(0.25 * inverse)
    out = []
    for stack in (forward, back):
        hi, lo = split_np(np.concatenate(stack))
        out.append(np.concatenate([hi, hi, lo], axis=1))
    return out


def split(value):
    hi = value.astype(BF16)
    lo = (value - hi.astype(F32)).astype(BF16)
    return hi, lo


def dot3(table_ref, part, value):
    hi, lo = split(value)
    both = jnp.concatenate([hi, lo, hi], axis=0)
    rows = table_ref[part * QUARTER : (part + 1) * QUARTER]
    return jnp.dot(rows, both, preferred_element_type=F32)


def transform(pieces, table_ref):
    one, two, three, four = pieces
    even, late = one + three, two + four
    odd, last = one - three, two - four
    third, fourth = last[:GROUP], last[GROUP:]
    plain = jnp.concatenate([odd[:GROUP] - third, odd[GROUP:] + fourth], axis=0)
    turned = ROOT * jnp.concatenate([fourth, -third], axis=0)
    residues = (even + late, even - late, plain - turned, plain + turned)
    return [dot3(table_ref, part, value) for part, value in enumerate(residues)]


def combine(parts):
    total, diff, left, right = parts
    plain = left + right
    turned = (left - right) * (1.0 / ROOT)
    third, fourth = turned[GROUP:], -turned[:GROUP]
    odd = jnp.concatenate([plain[:GROUP] + third, plain[GROUP:] - fourth], axis=0)
    last = jnp.concatenate([third, fourth], axis=0)
    return odd + (total + diff), last + (total - diff)


def name_channels(order_ref, group_ref, place_ref, high_ref, low_ref, names_ref):
    names_ref[...] = jnp.zeros_like(names_ref)
    names_ref[0, :SLOTS] = group_ref[...]
    names_ref[1, :SLOTS] = place_ref[...]
    blocks = high_ref.shape[0]
    width = blocks * BLOCK
    for row in range(0, blocks, 8):
        for col in range(0, width, GROUP):
            group = names_ref[0, row : row + 8, col : col + GROUP]
            place = names_ref[1, row : row + 8, col : col + GROUP]
            chan = jnp.zeros_like(place)
            for g in range(order_ref.shape[0]):
                names = jnp.broadcast_to(order_ref[g : g + 1, :], (8, GROUP))
                chan = jnp.where(group == g, lane_pick(names, place), chan)
            names_ref[0, row : row + 8, col : col + GROUP] = chan
    chan = names_ref[0]
    slot = lax.broadcasted_iota(jnp.int32, (blocks, LANES), 0)
    lane = lax.broadcasted_iota(jnp.int32, (blocks, LANES), 1)
    repeat = jnp.where(lax.shift_right_logical(lane, 3) == slot, 1.0, 0.0).astype(BF16)
    row = lax.broadcasted_iota(jnp.int32, (width, LANES), 0)
    lane = lax.broadcasted_iota(jnp.int32, (width, LANES), 1)
    own = jnp.bitwise_and(row, BLOCK - 1) == jnp.bitwise_and(lane, BLOCK - 1)
    for out_ref, part in (
        (high_ref, lax.shift_right_logical(chan, 8)),
        (low_ref, jnp.bitwise_and(chan, LANES - 1)),
    ):
        turned = part.astype(F32).T.astype(BF16)
        wide = jnp.dot(turned, repeat, preferred_element_type=F32)
        wide = jnp.where(own, wide, 0.0).reshape(blocks, BLOCK, LANES)
        out_ref[...] = jnp.sum(wide, axis=1).astype(jnp.int32)


def template_kernel(
    waves_ref, order_ref, group_ref, place_ref, table_ref, spec_ref, high_ref, low_ref, pad_ref, names_ref
):
    name_channels(order_ref, group_ref, place_ref, high_ref, low_ref, names_ref)
    pad_ref[...] = jnp.zeros_like(pad_ref)
    pad_ref[:USED, :TAPS] = waves_ref[...]
    waves = pad_ref[...].T
    mean = jnp.sum(waves * waves, axis=0, keepdims=True) * (1.0 / TAPS)
    scale = 1.0 / (jnp.sqrt(mean + 1e-6) * np.float32(np.sqrt(TAPS * SLOTS)))
    waves = waves * scale
    pieces = [waves[at : at + QUARTER] for at in range(0, 4 * QUARTER, QUARTER)]
    total, *rest = transform(pieces, table_ref)
    for part, spec in enumerate(rest):
        spec_ref[part * QUARTER : (part + 1) * QUARTER] = spec
    real, imag = total[:GROUP], total[GROUP:]
    first = lax.broadcasted_iota(jnp.int32, real.shape, 0) == 0
    at = 3 * QUARTER
    spec_ref[at : at + GROUP] = real
    spec_ref[at + GROUP : at + 2 * GROUP] = jnp.where(first, 0.0, imag)
    spec_ref[at + 2 * GROUP :] = jnp.where(first, imag, real)


def lane_pick(source, index):
    return jnp.take_along_axis(source, index, axis=1)


def select_kernel(record_ref, high_ref, low_ref, out_ref):
    blocks = high_ref.shape[0]
    span, channels = record_ref.shape
    width = LANES
    parts = []
    for at in range(0, channels, width):
        parts.extend(split(record_ref[:, at : at + width]))
    parts = jnp.concatenate(parts, axis=0)
    row = lax.broadcasted_iota(jnp.int32, (width, LANES), 0).astype(F32).astype(BF16)
    one, zero = jnp.ones((), BF16), jnp.zeros((), BF16)
    for block in range(blocks):
        high = high_ref[block : block + 1, :]
        low = low_ref[block : block + 1, :].astype(F32).astype(BF16)
        hot = jnp.where(row == low, one, zero)
        both = jnp.dot(parts, hot, preferred_element_type=F32)
        picked = jnp.zeros((span, LANES), F32)
        for g in range(channels // width):
            at = 2 * span * g
            quarter = both[at : at + span] + both[at + span : at + 2 * span]
            picked = jnp.where(high == g, quarter, picked)
        out_ref[block] = picked


def route(block, plane):
    low, core, z = block // 16, block // 8 % 2, block % 8
    far = plane ^ z
    key = (far & 1) * 7 ^ (far >> 1 & 1) * 5 ^ (far >> 2 & 1) ^ (3 * core)
    return (plane ^ key) * 4 + (low ^ (key & 1)) * 2 + core


def load_rows(recv_ref, plane, x_ref, first, count, at):
    span = recv_ref.shape[1]
    row = first
    while row < first + count:
        block, low = divmod(row, span)
        take = min(span - low, first + count - row)
        x_ref[at : at + take, :] = recv_ref[route(block, plane), low : low + take, :]
        row += take
        at += take


def ends_kernel(plane_ref, recv_ref, head_ref, tail_ref):
    plane = plane_ref[0]
    total = recv_ref.shape[0] * recv_ref.shape[1]
    load_rows(recv_ref, plane, head_ref, 0, NEXT, 0)
    load_rows(recv_ref, plane, tail_ref, total - BACK, BACK, 0)


def window_scale(x_ref, sq_ref, lags):
    span = TAPS // 8
    starts = lags // 8 + 1
    wide = 8 * starts

    def square(group):
        value = x_ref[8 * group : 8 * group + 8]
        return value * value

    for first in range(0, starts, 60):
        end = min(first + 60, starts)
        total = square(end - 1)
        for group in range(end, first + span):
            total = total + square(group)
        for group in range(end - 1, first - 1, -1):
            if group < end - 1:
                total = total + square(group)
            sq_ref[8 * group : 8 * group + 8] = total
        total = jnp.zeros((8, LANES), F32)
        for group in range(first + 1, end):
            total = total + square(group + span - 1)
            sq_ref[8 * group : 8 * group + 8] += total
    sq_ref[wide : wide + 8] = jnp.zeros((8, LANES), F32)
    for step in (1, 2, 4):
        total = sq_ref[:wide] + sq_ref[step : wide + step]
        if step < 4:
            sq_ref[:wide] = total
    return lax.rsqrt(total[:lags] * (1.0 / TAPS) + 1e-6)


def segments(x_ref, sq_ref, spans, spec_ref, forward_ref, back_ref):
    scale = window_scale(x_ref, sq_ref, sum(spans))
    stacks = []
    base = 0
    for lags in spans:
        pieces = [x_ref[at : at + QUARTER] for at in range(base, base + 4 * QUARTER, QUARTER)]
        spectra = transform(pieces, forward_ref)
        parts = []
        for part, spectrum in enumerate(spectra):
            real, imag = spectrum[:GROUP], spectrum[GROUP:]
            at = (part - 1) % 4 * QUARTER
            wave_real, wave_imag = spec_ref[at : at + GROUP], spec_ref[at + GROUP : at + QUARTER]
            wave_last = wave_real if part else spec_ref[at + QUARTER : at + QUARTER + GROUP]
            product = [real * wave_real + imag * wave_imag, imag * wave_last - real * wave_imag]
            parts.append(dot3(back_ref, part, jnp.concatenate(product, axis=0)))
        first, second = combine(parts)
        corr = jnp.concatenate([first, second[: lags - QUARTER]], axis=0)
        corr = corr * scale[base : base + lags]
        folded = (corr[:, :GROUP] + corr[:, GROUP:]).T
        acc = folded[:BLOCK]
        for s in range(1, GROUP // BLOCK):
            acc = acc + folded[s * BLOCK : (s + 1) * BLOCK]
        stacks.append(acc)
        base += lags
    return stacks


def near_kernel(plane_ref, recv_ref, *refs):
    *refs, out_ref, x_ref, sq_ref = refs
    load_rows(recv_ref, plane_ref[0], x_ref, KEEP, HOP + 2 * HALF, 0)
    one, two = segments(x_ref, sq_ref, (HOP, HOP), *refs)
    out_ref[:, :HOP] = one
    out_ref[:, HOP:] = two


def back_kernel(plane_ref, recv_ref, tail_ref, *refs):
    *refs, send_ref, keep_ref, x_ref, sq_ref = refs
    x_ref[:BACK] = tail_ref[...]
    load_rows(recv_ref, plane_ref[0], x_ref, 0, 2 * HALF - BACK, BACK)
    (stack,) = segments(x_ref, sq_ref, (BACK + KEEP,), *refs)
    send_ref[...] = stack[:, :BACK]
    keep_ref[...] = stack[:, BACK:]


def last_kernel(plane_ref, recv_ref, head_ref, *refs):
    *refs, out_ref, x_ref, sq_ref = refs
    own = recv_ref.shape[0] * recv_ref.shape[1] - KEEP - 2 * HOP
    load_rows(recv_ref, plane_ref[0], x_ref, KEEP + 2 * HOP, own, 0)
    x_ref[own : own + NEXT] = head_ref[...]
    x_ref[own + NEXT : 2 * HALF] = jnp.zeros((2 * HALF - own - NEXT, LANES), F32)
    (out_ref[...],) = segments(x_ref, sq_ref, (MOST,), *refs)


def join_kernel(*refs):
    *parts, out_ref = refs
    at = 0
    for part in parts:
        out_ref[:, at : at + part.shape[1]] = part[...]
        at += part.shape[1]


def call(kernel, out_shape, scratch, flops, nbytes, mib, name, scalars=0):
    def run(*operands):
        smem = pl.BlockSpec(memory_space=pltpu.SMEM)
        vmem = pl.BlockSpec(memory_space=pltpu.VMEM)
        return pl.pallas_call(
            kernel,
            out_shape=out_shape,
            in_specs=[smem if i < scalars else vmem for i in range(len(operands))],
            scratch_shapes=scratch,
            compiler_params=pltpu.CompilerParams(vmem_limit_bytes=mib << 20),
            cost_estimate=pl.CostEstimate(flops=flops, bytes_accessed=nbytes, transcendentals=0),
            name=name,
        )(*operands)

    return run


def shards(record, channel_order, templates, group_of_slot, place_of_slot):
    blocks = lax.axis_size("tmpl")
    planes = lax.axis_size("chan")
    span = record.shape[1]
    lags = blocks * span
    forward, back = (jnp.asarray(t) for t in tables())
    across, along = [], []
    per_plane = blocks // planes
    for b in range(blocks):
        for z in range(planes):
            plane, lane = divmod(b, per_plane)
            keeper = route(lane * planes + z, plane)
            across.append((b * planes + z, keeper * planes + z))
            along.append((keeper * planes + z, keeper * planes + plane))
    raw = lax.ppermute(record.T, ("tmpl", "chan"), across)
    plane = lax.axis_index("chan").astype(jnp.int32).reshape(1)

    waves = templates.transpose(1, 0, 2).reshape(USED, TAPS)
    small = (
        waves,
        channel_order.reshape(-1, GROUP),
        group_of_slot.reshape(-1, SLOTS).T,
        place_of_slot.T,
    )
    raw, plane, small = lax.optimization_barrier((raw, plane, small))
    raw = lax.ppermute(raw, ("tmpl", "chan"), along)
    names = jax.ShapeDtypeStruct((blocks, LANES), jnp.int32)
    specs, high, low = call(
        template_kernel,
        (jax.ShapeDtypeStruct((3 * QUARTER + 3 * GROUP, LANES), F32), names, names),
        [
            pltpu.VMEM((LANES, 4 * QUARTER), F32),
            pltpu.VMEM((2, blocks, blocks * BLOCK), jnp.int32),
        ],
        2 * 3 * 4 * QUARTER * QUARTER * LANES,
        4 << 20,
        16,
        "template_spectra",
    )(*small, forward)
    raw, high, low, specs = lax.optimization_barrier((raw, high, low, specs))
    sent = call(
        select_kernel,
        jax.ShapeDtypeStruct((blocks, span, LANES), F32),
        [],
        1 << 20,
        4 << 20,
        8,
        "select_channels",
    )(raw, high, low)
    recv = lax.all_to_all(sent, "tmpl", split_axis=0, concat_axis=0, tiled=True)
    rows = jax.ShapeDtypeStruct((BACK, LANES), F32), jax.ShapeDtypeStruct((NEXT, LANES), F32)
    head, tail = call(ends_kernel, rows[::-1], [], 0, 1 << 20, 8, "ends", 1)(plane, recv)
    up = [(z, (z + 1) % planes) for z in range(planes)]
    down = [(t, s) for s, t in up]
    after = lax.ppermute(head, "chan", down)
    before = lax.ppermute(tail, "chan", up)
    flops = 2 * 3 * (2 * HALF * HALF + HOP * 2 * HALF) * LANES
    shared = (specs, forward, back)

    def part(kernel, count, name, *lags):
        lines = pltpu.VMEM(((count - 1) * HOP + 2 * HALF + 8, LANES), F32)
        shape = tuple(jax.ShapeDtypeStruct((BLOCK, n), F32) for n in lags)
        return call(kernel, shape, [lines, lines], count * flops, 8 << 20, 24, name, 1)

    (middle,) = part(near_kernel, 2, "near_segments", 2 * HOP)(plane, recv, *shared)
    early, keep = part(back_kernel, 1, "back_segment", BACK, KEEP)(plane, recv, before, *shared)
    given = lax.ppermute(early, "chan", down)
    (last,) = part(last_kernel, 1, "last_segment", MOST)(plane, recv, after, *shared)
    joined = jax.ShapeDtypeStruct((BLOCK, blocks * span), F32)
    return call(join_kernel, joined, [], 0, 1 << 17, 8, "join")(keep, middle, last, given)


def solution(mesh):
    placed = (P(None, ("tmpl", "chan")), P(), P("tmpl", None, None), P(), P())
    return jax.shard_map(
        shards, mesh=mesh, in_specs=placed, out_specs=P("tmpl", "chan"), check_vma=False
    )
```

```python
import jax
import jax.numpy as jnp
import ml_dtypes
import numpy as np
from jax import lax
from jax.experimental import pallas as pl
from jax.experimental.pallas import tpu as pltpu
from jax.sharding import PartitionSpec as P

SLOTS = 30
TAPS = 600
BLOCK = 8
LANES = 256
USED = SLOTS * BLOCK
HALF = 512
HOP = 384
MOST = 408
GROUP = 128
QUARTER = 256
ROOT = float(np.sqrt(2.0))
BACK = 232
KEEP = 128
NEXT = 368

F32 = jnp.float32
BF16 = jnp.bfloat16


def split_np(table):
    hi = table.astype(ml_dtypes.bfloat16)
    lo = (table - hi.astype(np.float64)).astype(ml_dtypes.bfloat16)
    return hi, lo


def tables():
    n = np.arange(QUARTER, dtype=np.int64)[None, :]
    m = np.arange(GROUP, dtype=np.int64)[:, None]
    forward, back = [], []
    for eighths in (0, 4, 1, 3):
        if eighths in (0, 4):
            angle = ((2 * m + eighths // 4) * n % (2 * QUARTER)) * (np.pi / QUARTER)
            imag = -np.sin(angle)
            weight = np.full((QUARTER, 1), 2.0 / QUARTER)
            if not eighths:
                imag[0] = 1.0 - 2.0 * (n[0] % 2)
                weight[0] = weight[GROUP] = 1.0 / QUARTER
            table = np.concatenate([np.cos(angle), imag])
            inverse = (weight * table).T
        else:
            angle = ((8 * m + eighths) * n % (8 * GROUP)) * (np.pi / (4 * GROUP))
            table = np.concatenate([np.cos(angle), -np.sin(angle)])
            sign = 1.0 if eighths == 1 else -1.0
            cos, sin = np.cos(angle[:, :GROUP]).T / GROUP, np.sin(angle[:, :GROUP]).T / GROUP
            root = np.sqrt(2.0)
            low = np.concatenate([cos + sign * sin, sign * cos - sin], axis=1)
            high = np.concatenate([-root * sin, -root * cos], axis=1)
            inverse = np.concatenate([low, high])
        forward.append(table)
        back.append(0.25 * inverse)
    out = []
    for stack in (forward, back):
        hi, lo = split_np(np.concatenate(stack))
        out.append(np.concatenate([hi, hi, lo], axis=1))
    return out


def split(value):
    hi = value.astype(BF16)
    lo = (value - hi.astype(F32)).astype(BF16)
    return hi, lo


def dot3(table_ref, part, value):
    hi, lo = split(value)
    both = jnp.concatenate([hi, lo, hi], axis=0)
    rows = table_ref[part * QUARTER : (part + 1) * QUARTER]
    return jnp.dot(rows, both, preferred_element_type=F32)


def transform(pieces, table_ref):
    one, two, three, four = pieces
    even, late = one + three, two + four
    odd, last = one - three, two - four
    third, fourth = last[:GROUP], last[GROUP:]
    plain = jnp.concatenate([odd[:GROUP] - third, odd[GROUP:] + fourth], axis=0)
    turned = ROOT * jnp.concatenate([fourth, -third], axis=0)
    residues = (even + late, even - late, plain - turned, plain + turned)
    return [dot3(table_ref, part, value) for part, value in enumerate(residues)]


def combine(parts):
    total, diff, left, right = parts
    plain = left + right
    turned = (left - right) * (1.0 / ROOT)
    third, fourth = turned[GROUP:], -turned[:GROUP]
    odd = jnp.concatenate([plain[:GROUP] + third, plain[GROUP:] - fourth], axis=0)
    last = jnp.concatenate([third, fourth], axis=0)
    return odd + (total + diff), last + (total - diff)


def name_channels(order_ref, group_ref, place_ref, high_ref, low_ref, names_ref):
    names_ref[...] = jnp.zeros_like(names_ref)
    names_ref[0, :SLOTS] = group_ref[...]
    names_ref[1, :SLOTS] = place_ref[...]
    blocks = high_ref.shape[0]
    width = blocks * BLOCK
    for row in range(0, blocks, 8):
        for col in range(0, width, GROUP):
            group = names_ref[0, row : row + 8, col : col + GROUP]
            place = names_ref[1, row : row + 8, col : col + GROUP]
            chan = jnp.zeros_like(place)
            for g in range(order_ref.shape[0]):
                names = jnp.broadcast_to(order_ref[g : g + 1, :], (8, GROUP))
                chan = jnp.where(group == g, lane_pick(names, place), chan)
            names_ref[0, row : row + 8, col : col + GROUP] = chan
    chan = names_ref[0]
    slot = lax.broadcasted_iota(jnp.int32, (blocks, LANES), 0)
    lane = lax.broadcasted_iota(jnp.int32, (blocks, LANES), 1)
    repeat = jnp.where(lax.shift_right_logical(lane, 3) == slot, 1.0, 0.0).astype(BF16)
    row = lax.broadcasted_iota(jnp.int32, (width, LANES), 0)
    lane = lax.broadcasted_iota(jnp.int32, (width, LANES), 1)
    own = jnp.bitwise_and(row, BLOCK - 1) == jnp.bitwise_and(lane, BLOCK - 1)
    for out_ref, part in (
        (high_ref, lax.shift_right_logical(chan, 8)),
        (low_ref, jnp.bitwise_and(chan, LANES - 1)),
    ):
        turned = part.astype(F32).T.astype(BF16)
        wide = jnp.dot(turned, repeat, preferred_element_type=F32)
        wide = jnp.where(own, wide, 0.0).reshape(blocks, BLOCK, LANES)
        out_ref[...] = jnp.sum(wide, axis=1).astype(jnp.int32)


def template_kernel(
    waves_ref, order_ref, group_ref, place_ref, table_ref, spec_ref, high_ref, low_ref, pad_ref, names_ref
):
    name_channels(order_ref, group_ref, place_ref, high_ref, low_ref, names_ref)
    pad_ref[...] = jnp.zeros_like(pad_ref)
    pad_ref[:USED, :TAPS] = waves_ref[...]
    waves = pad_ref[...].T
    mean = jnp.sum(waves * waves, axis=0, keepdims=True) * (1.0 / TAPS)
    scale = 1.0 / (jnp.sqrt(mean + 1e-6) * np.float32(np.sqrt(TAPS * SLOTS)))
    waves = waves * scale
    pieces = [waves[at : at + QUARTER] for at in range(0, 4 * QUARTER, QUARTER)]
    total, *rest = transform(pieces, table_ref)
    for part, spec in enumerate(rest):
        spec_ref[part * QUARTER : (part + 1) * QUARTER] = spec
    real, imag = total[:GROUP], total[GROUP:]
    first = lax.broadcasted_iota(jnp.int32, real.shape, 0) == 0
    at = 3 * QUARTER
    spec_ref[at : at + GROUP] = real
    spec_ref[at + GROUP : at + 2 * GROUP] = jnp.where(first, 0.0, imag)
    spec_ref[at + 2 * GROUP :] = jnp.where(first, imag, real)


def lane_pick(source, index):
    return jnp.take_along_axis(source, index, axis=1)


def select_kernel(record_ref, high_ref, low_ref, out_ref):
    blocks = high_ref.shape[0]
    span, channels = record_ref.shape
    width = LANES
    parts = []
    for at in range(0, channels, width):
        parts.extend(split(record_ref[:, at : at + width]))
    parts = jnp.concatenate(parts, axis=0)
    row = lax.broadcasted_iota(jnp.int32, (width, LANES), 0).astype(F32).astype(BF16)
    one, zero = jnp.ones((), BF16), jnp.zeros((), BF16)
    for block in range(blocks):
        high = high_ref[block : block + 1, :]
        low = low_ref[block : block + 1, :].astype(F32).astype(BF16)
        hot = jnp.where(row == low, one, zero)
        both = jnp.dot(parts, hot, preferred_element_type=F32)
        picked = jnp.zeros((span, LANES), F32)
        for g in range(channels // width):
            at = 2 * span * g
            quarter = both[at : at + span] + both[at + span : at + 2 * span]
            picked = jnp.where(high == g, quarter, picked)
        out_ref[block] = picked


def route(block, plane):
    low, core, z = block // 16, block // 8 % 2, block % 8
    far = plane ^ z
    key = (far & 1) * 7 ^ (far >> 1 & 1) * 5 ^ (far >> 2 & 1) ^ (3 * core)
    return (plane ^ key) * 4 + (low ^ (key & 1)) * 2 + core


def load_rows(recv_ref, plane, x_ref, first, count, at):
    span = recv_ref.shape[1]
    row = first
    while row < first + count:
        block, low = divmod(row, span)
        take = min(span - low, first + count - row)
        x_ref[at : at + take, :] = recv_ref[route(block, plane), low : low + take, :]
        row += take
        at += take


def ends_kernel(plane_ref, recv_ref, head_ref, tail_ref):
    plane = plane_ref[0]
    total = recv_ref.shape[0] * recv_ref.shape[1]
    load_rows(recv_ref, plane, head_ref, 0, NEXT, 0)
    load_rows(recv_ref, plane, tail_ref, total - BACK, BACK, 0)


def window_scale(rows, sq_ref, lags):
    span = TAPS // 8
    starts = lags // 8 + 1
    wide = 8 * starts

    def square(group):
        value = rows(8 * group, 8)
        return value * value

    for first in range(0, starts, 60):
        end = min(first + 60, starts)
        total = square(end - 1)
        for group in range(end, first + span):
            total = total + square(group)
        for group in range(end - 1, first - 1, -1):
            if group < end - 1:
                total = total + square(group)
            sq_ref[8 * group : 8 * group + 8] = total
        total = jnp.zeros((8, LANES), F32)
        for group in range(first + 1, end):
            total = total + square(group + span - 1)
            sq_ref[8 * group : 8 * group + 8] += total
    sq_ref[wide : wide + 8] = jnp.zeros((8, LANES), F32)
    for step in (1, 2, 4):
        total = sq_ref[:wide] + sq_ref[step : wide + step]
        if step < 4:
            sq_ref[:wide] = total
    return lax.rsqrt(total[:lags] * (1.0 / TAPS) + 1e-6)


def segments(rows, sq_ref, spans, spec_ref, forward_ref, back_ref):
    scale = window_scale(rows, sq_ref, sum(spans))
    stacks = []
    base = 0
    for lags in spans:
        pieces = [rows(at, QUARTER) for at in range(base, base + 4 * QUARTER, QUARTER)]
        spectra = transform(pieces, forward_ref)
        parts = []
        for part, spectrum in enumerate(spectra):
            real, imag = spectrum[:GROUP], spectrum[GROUP:]
            at = (part - 1) % 4 * QUARTER
            wave_real, wave_imag = spec_ref[at : at + GROUP], spec_ref[at + GROUP : at + QUARTER]
            wave_last = wave_real if part else spec_ref[at + QUARTER : at + QUARTER + GROUP]
            product = [real * wave_real + imag * wave_imag, imag * wave_last - real * wave_imag]
            parts.append(dot3(back_ref, part, jnp.concatenate(product, axis=0)))
        first, second = combine(parts)
        corr = jnp.concatenate([first, second[: lags - QUARTER]], axis=0)
        corr = corr * scale[base : base + lags]
        folded = (corr[:, :GROUP] + corr[:, GROUP:]).T
        acc = folded[:BLOCK]
        for s in range(1, GROUP // BLOCK):
            acc = acc + folded[s * BLOCK : (s + 1) * BLOCK]
        stacks.append(acc)
        base += lags
    return stacks


def chained(refs, first):
    def rows(at, count):
        at += first
        parts = []
        for ref in refs:
            size = ref.shape[0]
            low, high = min(at, size), min(at + count, size)
            if low < high:
                parts.append(ref[low:high])
                count -= high - low
            at = max(at - size, 0)
        if count:
            parts.append(jnp.zeros((count, LANES), F32))
        return parts[0] if len(parts) == 1 else jnp.concatenate(parts, axis=0)

    return rows


def near_kernel(plane_ref, recv_ref, *refs):
    *refs, out_ref, x_ref, sq_ref = refs
    load_rows(recv_ref, plane_ref[0], x_ref, 0, x_ref.shape[0], 0)
    one, two = segments(chained([x_ref], KEEP), sq_ref, (HOP, HOP), *refs)
    out_ref[:, :HOP] = one
    out_ref[:, HOP:] = two


def back_kernel(x_ref, tail_ref, *refs):
    *refs, send_ref, keep_ref, sq_ref = refs
    (stack,) = segments(chained([tail_ref, x_ref], 0), sq_ref, (BACK + KEEP,), *refs)
    send_ref[...] = stack[:, :BACK]
    keep_ref[...] = stack[:, BACK:]


def last_kernel(x_ref, head_ref, *refs):
    *refs, out_ref, sq_ref = refs
    rows = chained([x_ref, head_ref], KEEP + 2 * HOP)
    (out_ref[...],) = segments(rows, sq_ref, (MOST,), *refs)


def join_kernel(*refs):
    *parts, out_ref = refs
    at = 0
    for part in parts:
        out_ref[:, at : at + part.shape[1]] = part[...]
        at += part.shape[1]


def call(kernel, out_shape, scratch, flops, nbytes, mib, name, scalars=0):
    def run(*operands):
        smem = pl.BlockSpec(memory_space=pltpu.SMEM)
        vmem = pl.BlockSpec(memory_space=pltpu.VMEM)
        return pl.pallas_call(
            kernel,
            out_shape=out_shape,
            in_specs=[smem if i < scalars else vmem for i in range(len(operands))],
            scratch_shapes=scratch,
            compiler_params=pltpu.CompilerParams(vmem_limit_bytes=mib << 20),
            cost_estimate=pl.CostEstimate(flops=flops, bytes_accessed=nbytes, transcendentals=0),
            name=name,
        )(*operands)

    return run


def shards(record, channel_order, templates, group_of_slot, place_of_slot):
    blocks = lax.axis_size("tmpl")
    planes = lax.axis_size("chan")
    span = record.shape[1]
    lags = blocks * span
    forward, back = (jnp.asarray(t) for t in tables())
    across, along = [], []
    per_plane = blocks // planes
    for b in range(blocks):
        for z in range(planes):
            plane, lane = divmod(b, per_plane)
            keeper = route(lane * planes + z, plane)
            across.append((b * planes + z, keeper * planes + z))
            along.append((keeper * planes + z, keeper * planes + plane))
    raw = lax.ppermute(record.T, ("tmpl", "chan"), across)
    plane = lax.axis_index("chan").astype(jnp.int32).reshape(1)

    waves = templates.transpose(1, 0, 2).reshape(USED, TAPS)
    small = (
        waves,
        channel_order.reshape(-1, GROUP),
        group_of_slot.reshape(-1, SLOTS).T,
        place_of_slot.T,
    )
    raw, plane, small = lax.optimization_barrier((raw, plane, small))
    raw = lax.ppermute(raw, ("tmpl", "chan"), along)
    names = jax.ShapeDtypeStruct((blocks, LANES), jnp.int32)
    specs, high, low = call(
        template_kernel,
        (jax.ShapeDtypeStruct((3 * QUARTER + 3 * GROUP, LANES), F32), names, names),
        [
            pltpu.VMEM((LANES, 4 * QUARTER), F32),
            pltpu.VMEM((2, blocks, blocks * BLOCK), jnp.int32),
        ],
        2 * 3 * 4 * QUARTER * QUARTER * LANES,
        4 << 20,
        16,
        "template_spectra",
    )(*small, forward)
    raw, high, low, specs = lax.optimization_barrier((raw, high, low, specs))
    sent = call(
        select_kernel,
        jax.ShapeDtypeStruct((blocks, span, LANES), F32),
        [],
        1 << 20,
        4 << 20,
        8,
        "select_channels",
    )(raw, high, low)
    recv = lax.all_to_all(sent, "tmpl", split_axis=0, concat_axis=0, tiled=True)
    rows = jax.ShapeDtypeStruct((BACK, LANES), F32), jax.ShapeDtypeStruct((NEXT, LANES), F32)
    head, tail = call(ends_kernel, rows[::-1], [], 0, 1 << 20, 8, "ends", 1)(plane, recv)
    up = [(z, (z + 1) % planes) for z in range(planes)]
    down = [(t, s) for s, t in up]
    after = lax.ppermute(head, "chan", down)
    before = lax.ppermute(tail, "chan", up)
    flops = 2 * 3 * (2 * HALF * HALF + HOP * 2 * HALF) * LANES
    shared = (specs, forward, back)

    def part(kernel, count, name, scalars, *shapes):
        shapes = tuple(jax.ShapeDtypeStruct(shape, F32) for shape in shapes)
        sums = [pltpu.VMEM((count * MOST + 16, LANES), F32)]
        return call(kernel, shapes, sums, count * flops, 8 << 20, 24, name, scalars)

    middle, own = part(
        near_kernel, 2, "near_segments", 1, (BLOCK, 2 * HOP), (blocks * span, LANES)
    )(plane, recv, *shared)
    early, keep = part(back_kernel, 1, "back_segment", 0, (BLOCK, BACK), (BLOCK, KEEP))(
        own, before, *shared
    )
    given = lax.ppermute(early, "chan", down)
    (last,) = part(last_kernel, 1, "last_segment", 0, (BLOCK, MOST))(own, after, *shared)
    joined = jax.ShapeDtypeStruct((BLOCK, blocks * span), F32)
    return call(join_kernel, joined, [], 0, 1 << 17, 8, "join")(keep, middle, last, given)


def solution(mesh):
    placed = (P(None, ("tmpl", "chan")), P(), P("tmpl", None, None), P(), P())
    return jax.shard_map(
        shards, mesh=mesh, in_specs=placed, out_specs=P("tmpl", "chan"), check_vma=False
    )
```

```python
import jax
import jax.numpy as jnp
import ml_dtypes
import numpy as np
from jax import lax
from jax.experimental import pallas as pl
from jax.experimental.pallas import tpu as pltpu
from jax.sharding import PartitionSpec as P

SLOTS = 30
TAPS = 600
BLOCK = 8
LANES = 256
USED = SLOTS * BLOCK
HALF = 512
HOP = 384
MOST = 408
GROUP = 128
QUARTER = 256
ROOT = float(np.sqrt(2.0))
BACK = 232
KEEP = 128
NEXT = 368

F32 = jnp.float32
BF16 = jnp.bfloat16


def split_np(table):
    hi = table.astype(ml_dtypes.bfloat16)
    lo = (table - hi.astype(np.float64)).astype(ml_dtypes.bfloat16)
    return hi, lo


def tables():
    n = np.arange(QUARTER, dtype=np.int64)[None, :]
    m = np.arange(GROUP, dtype=np.int64)[:, None]
    forward, back = [], []
    for eighths in (0, 4, 1, 3):
        if eighths in (0, 4):
            angle = ((2 * m + eighths // 4) * n % (2 * QUARTER)) * (np.pi / QUARTER)
            imag = -np.sin(angle)
            weight = np.full((QUARTER, 1), 2.0 / QUARTER)
            if not eighths:
                imag[0] = 1.0 - 2.0 * (n[0] % 2)
                weight[0] = weight[GROUP] = 1.0 / QUARTER
            table = np.concatenate([np.cos(angle), imag])
            inverse = (weight * table).T
        else:
            angle = ((8 * m + eighths) * n % (8 * GROUP)) * (np.pi / (4 * GROUP))
            table = np.concatenate([np.cos(angle), -np.sin(angle)])
            sign = 1.0 if eighths == 1 else -1.0
            cos, sin = np.cos(angle[:, :GROUP]).T / GROUP, np.sin(angle[:, :GROUP]).T / GROUP
            root = np.sqrt(2.0)
            low = np.concatenate([cos + sign * sin, sign * cos - sin], axis=1)
            high = np.concatenate([-root * sin, -root * cos], axis=1)
            inverse = np.concatenate([low, high])
        forward.append(table)
        back.append(0.25 * inverse)
    out = []
    for stack in (forward, back):
        hi, lo = split_np(np.concatenate(stack))
        out.append(np.concatenate([hi, hi, lo], axis=1))
    return out


def split(value):
    hi = value.astype(BF16)
    lo = (value - hi.astype(F32)).astype(BF16)
    return hi, lo


def dot3(table_ref, part, value):
    hi, lo = split(value)
    both = jnp.concatenate([hi, lo, hi], axis=0)
    rows = table_ref[part * QUARTER : (part + 1) * QUARTER]
    return jnp.dot(rows, both, preferred_element_type=F32)


def transform(pieces, table_ref):
    one, two, three, four = pieces
    even, late = one + three, two + four
    odd, last = one - three, two - four
    third, fourth = last[:GROUP], last[GROUP:]
    plain = jnp.concatenate([odd[:GROUP] - third, odd[GROUP:] + fourth], axis=0)
    turned = ROOT * jnp.concatenate([fourth, -third], axis=0)
    residues = (even + late, even - late, plain - turned, plain + turned)
    return [dot3(table_ref, part, value) for part, value in enumerate(residues)]


def combine(parts):
    total, diff, left, right = parts
    plain = left + right
    turned = (left - right) * (1.0 / ROOT)
    third, fourth = turned[GROUP:], -turned[:GROUP]
    odd = jnp.concatenate([plain[:GROUP] + third, plain[GROUP:] - fourth], axis=0)
    last = jnp.concatenate([third, fourth], axis=0)
    return odd + (total + diff), last + (total - diff)


def name_channels(order_ref, group_ref, place_ref, high_ref, low_ref, names_ref):
    names_ref[...] = jnp.zeros_like(names_ref)
    names_ref[0, :SLOTS] = group_ref[...]
    names_ref[1, :SLOTS] = place_ref[...]
    blocks = high_ref.shape[0]
    width = blocks * BLOCK
    for row in range(0, blocks, 8):
        for col in range(0, width, GROUP):
            group = names_ref[0, row : row + 8, col : col + GROUP]
            place = names_ref[1, row : row + 8, col : col + GROUP]
            chan = jnp.zeros_like(place)
            for g in range(order_ref.shape[0]):
                names = jnp.broadcast_to(order_ref[g : g + 1, :], (8, GROUP))
                chan = jnp.where(group == g, lane_pick(names, place), chan)
            names_ref[0, row : row + 8, col : col + GROUP] = chan
    chan = names_ref[0]
    slot = lax.broadcasted_iota(jnp.int32, (blocks, LANES), 0)
    lane = lax.broadcasted_iota(jnp.int32, (blocks, LANES), 1)
    repeat = jnp.where(lax.shift_right_logical(lane, 3) == slot, 1.0, 0.0).astype(BF16)
    row = lax.broadcasted_iota(jnp.int32, (width, LANES), 0)
    lane = lax.broadcasted_iota(jnp.int32, (width, LANES), 1)
    own = jnp.bitwise_and(row, BLOCK - 1) == jnp.bitwise_and(lane, BLOCK - 1)
    for out_ref, part in (
        (high_ref, lax.shift_right_logical(chan, 8)),
        (low_ref, jnp.bitwise_and(chan, LANES - 1)),
    ):
        turned = part.astype(F32).T.astype(BF16)
        wide = jnp.dot(turned, repeat, preferred_element_type=F32)
        wide = jnp.where(own, wide, 0.0).reshape(blocks, BLOCK, LANES)
        out_ref[...] = jnp.sum(wide, axis=1).astype(jnp.int32)


def template_kernel(
    waves_ref, order_ref, group_ref, place_ref, table_ref, spec_ref, high_ref, low_ref, pad_ref, names_ref
):
    name_channels(order_ref, group_ref, place_ref, high_ref, low_ref, names_ref)
    pad_ref[...] = jnp.zeros_like(pad_ref)
    pad_ref[:USED, :TAPS] = waves_ref[...]
    waves = pad_ref[...].T
    mean = jnp.sum(waves * waves, axis=0, keepdims=True) * (1.0 / TAPS)
    scale = 1.0 / (jnp.sqrt(mean + 1e-6) * np.float32(np.sqrt(TAPS * SLOTS)))
    waves = waves * scale
    pieces = [waves[at : at + QUARTER] for at in range(0, 4 * QUARTER, QUARTER)]
    total, *rest = transform(pieces, table_ref)
    for part, spec in enumerate(rest):
        spec_ref[part * QUARTER : (part + 1) * QUARTER] = spec
    real, imag = total[:GROUP], total[GROUP:]
    first = lax.broadcasted_iota(jnp.int32, real.shape, 0) == 0
    at = 3 * QUARTER
    spec_ref[at : at + GROUP] = real
    spec_ref[at + GROUP : at + 2 * GROUP] = jnp.where(first, 0.0, imag)
    spec_ref[at + 2 * GROUP :] = jnp.where(first, imag, real)


def lane_pick(source, index):
    return jnp.take_along_axis(source, index, axis=1)


def select_kernel(record_ref, high_ref, low_ref, out_ref):
    blocks = high_ref.shape[0]
    span, channels = record_ref.shape
    width = LANES
    parts = []
    for at in range(0, channels, width):
        parts.extend(split(record_ref[:, at : at + width]))
    parts = jnp.concatenate(parts, axis=0)
    row = lax.broadcasted_iota(jnp.int32, (width, LANES), 0).astype(F32).astype(BF16)
    one, zero = jnp.ones((), BF16), jnp.zeros((), BF16)
    for block in range(blocks):
        high = high_ref[block : block + 1, :]
        low = low_ref[block : block + 1, :].astype(F32).astype(BF16)
        hot = jnp.where(row == low, one, zero)
        both = jnp.dot(parts, hot, preferred_element_type=F32)
        quarters = [
            both[at : at + span] + both[at + span : at + 2 * span]
            for at in range(0, both.shape[0], 2 * span)
        ]
        odd, late = jnp.bitwise_and(high, 1) == 1, high >= 2
        early = jnp.where(odd, quarters[1], quarters[0])
        picked = jnp.where(late, jnp.where(odd, quarters[3], quarters[2]), early)
        out_ref[block] = picked


def route(block, plane):
    low, core, z = block // 16, block // 8 % 2, block % 8
    far = plane ^ z
    key = (far & 1) * 7 ^ (far >> 1 & 1) * 5 ^ (far >> 2 & 1) ^ (3 * core)
    return (plane ^ key) * 4 + (low ^ (key & 1)) * 2 + core


def load_rows(recv_ref, plane, x_ref, first, count, at):
    span = recv_ref.shape[1]
    row = first
    while row < first + count:
        block, low = divmod(row, span)
        take = min(span - low, first + count - row)
        x_ref[at : at + take, :] = recv_ref[route(block, plane), low : low + take, :]
        row += take
        at += take


def ends_kernel(plane_ref, recv_ref, head_ref, tail_ref):
    plane = plane_ref[0]
    total = recv_ref.shape[0] * recv_ref.shape[1]
    load_rows(recv_ref, plane, head_ref, 0, NEXT, 0)
    load_rows(recv_ref, plane, tail_ref, total - BACK, BACK, 0)


def window_scale(rows, sq_ref, lags):
    span = TAPS // 8
    starts = lags // 8 + 1
    wide = 8 * starts

    def square(group):
        value = rows(8 * group, 8)
        return value * value

    for first in range(0, starts, 60):
        end = min(first + 60, starts)
        total = square(end - 1)
        for group in range(end, first + span):
            total = total + square(group)
        for group in range(end - 1, first - 1, -1):
            if group < end - 1:
                total = total + square(group)
            sq_ref[8 * group : 8 * group + 8] = total
        total = jnp.zeros((8, LANES), F32)
        for group in range(first + 1, end):
            total = total + square(group + span - 1)
            sq_ref[8 * group : 8 * group + 8] += total
    sq_ref[wide : wide + 8] = jnp.zeros((8, LANES), F32)
    for step in (1, 2, 4):
        total = sq_ref[:wide] + sq_ref[step : wide + step]
        if step < 4:
            sq_ref[:wide] = total
    return lax.rsqrt(total[:lags] * (1.0 / TAPS) + 1e-6)


def segments(rows, sq_ref, spans, spec_ref, forward_ref, back_ref):
    scale = window_scale(rows, sq_ref, sum(spans))
    stacks = []
    base = 0
    for lags in spans:
        pieces = [rows(at, QUARTER) for at in range(base, base + 4 * QUARTER, QUARTER)]
        spectra = transform(pieces, forward_ref)
        parts = []
        for part, spectrum in enumerate(spectra):
            real, imag = spectrum[:GROUP], spectrum[GROUP:]
            at = (part - 1) % 4 * QUARTER
            wave_real, wave_imag = spec_ref[at : at + GROUP], spec_ref[at + GROUP : at + QUARTER]
            wave_last = wave_real if part else spec_ref[at + QUARTER : at + QUARTER + GROUP]
            product = [real * wave_real + imag * wave_imag, imag * wave_last - real * wave_imag]
            parts.append(dot3(back_ref, part, jnp.concatenate(product, axis=0)))
        first, second = combine(parts)
        corr = jnp.concatenate([first, second[: lags - QUARTER]], axis=0)
        corr = corr * scale[base : base + lags]
        folded = (corr[:, :GROUP] + corr[:, GROUP:]).T
        acc = folded[:BLOCK]
        for s in range(1, GROUP // BLOCK):
            acc = acc + folded[s * BLOCK : (s + 1) * BLOCK]
        stacks.append(acc)
        base += lags
    return stacks


def chained(refs, first):
    def rows(at, count):
        at += first
        parts = []
        for ref in refs:
            size = ref.shape[0]
            low, high = min(at, size), min(at + count, size)
            if low < high:
                parts.append(ref[low:high])
                count -= high - low
            at = max(at - size, 0)
        if count:
            parts.append(jnp.zeros((count, LANES), F32))
        return parts[0] if len(parts) == 1 else jnp.concatenate(parts, axis=0)

    return rows


def near_kernel(plane_ref, recv_ref, *refs):
    *refs, out_ref, x_ref, sq_ref = refs
    load_rows(recv_ref, plane_ref[0], x_ref, 0, x_ref.shape[0], 0)
    one, two = segments(chained([x_ref], KEEP), sq_ref, (HOP, HOP), *refs)
    out_ref[:, :HOP] = one
    out_ref[:, HOP:] = two


def back_kernel(x_ref, tail_ref, *refs):
    *refs, send_ref, keep_ref, sq_ref = refs
    (stack,) = segments(chained([tail_ref, x_ref], 0), sq_ref, (BACK + KEEP,), *refs)
    send_ref[...] = stack[:, :BACK]
    keep_ref[...] = stack[:, BACK:]


def last_kernel(x_ref, head_ref, *refs):
    *refs, out_ref, sq_ref = refs
    rows = chained([x_ref, head_ref], KEEP + 2 * HOP)
    (out_ref[...],) = segments(rows, sq_ref, (MOST,), *refs)


def join_kernel(*refs):
    *parts, out_ref = refs
    at = 0
    for part in parts:
        out_ref[:, at : at + part.shape[1]] = part[...]
        at += part.shape[1]


def call(kernel, out_shape, scratch, flops, nbytes, mib, name, scalars=0):
    def run(*operands):
        smem = pl.BlockSpec(memory_space=pltpu.SMEM)
        vmem = pl.BlockSpec(memory_space=pltpu.VMEM)
        return pl.pallas_call(
            kernel,
            out_shape=out_shape,
            in_specs=[smem if i < scalars else vmem for i in range(len(operands))],
            scratch_shapes=scratch,
            compiler_params=pltpu.CompilerParams(vmem_limit_bytes=mib << 20),
            cost_estimate=pl.CostEstimate(flops=flops, bytes_accessed=nbytes, transcendentals=0),
            name=name,
        )(*operands)

    return run


def shards(record, channel_order, templates, group_of_slot, place_of_slot):
    blocks = lax.axis_size("tmpl")
    planes = lax.axis_size("chan")
    span = record.shape[1]
    lags = blocks * span
    forward, back = (jnp.asarray(t) for t in tables())
    across, along = [], []
    per_plane = blocks // planes
    for b in range(blocks):
        for z in range(planes):
            plane, lane = divmod(b, per_plane)
            keeper = route(lane * planes + z, plane)
            across.append((b * planes + z, keeper * planes + z))
            along.append((keeper * planes + z, keeper * planes + plane))
    raw = lax.ppermute(record.T, ("tmpl", "chan"), across)
    plane = lax.axis_index("chan").astype(jnp.int32).reshape(1)

    waves = templates.transpose(1, 0, 2).reshape(USED, TAPS)
    small = (
        waves,
        channel_order.reshape(-1, GROUP),
        group_of_slot.reshape(-1, SLOTS).T,
        place_of_slot.T,
    )
    raw, plane, small = lax.optimization_barrier((raw, plane, small))
    raw = lax.ppermute(raw, ("tmpl", "chan"), along)
    names = jax.ShapeDtypeStruct((blocks, LANES), jnp.int32)
    specs, high, low = call(
        template_kernel,
        (jax.ShapeDtypeStruct((3 * QUARTER + 3 * GROUP, LANES), F32), names, names),
        [
            pltpu.VMEM((LANES, 4 * QUARTER), F32),
            pltpu.VMEM((2, blocks, blocks * BLOCK), jnp.int32),
        ],
        2 * 3 * 4 * QUARTER * QUARTER * LANES,
        4 << 20,
        16,
        "template_spectra",
    )(*small, forward)
    raw, high, low, specs = lax.optimization_barrier((raw, high, low, specs))
    sent = call(
        select_kernel,
        jax.ShapeDtypeStruct((blocks, span, LANES), F32),
        [],
        1 << 20,
        4 << 20,
        8,
        "select_channels",
    )(raw, high, low)
    recv = lax.all_to_all(sent, "tmpl", split_axis=0, concat_axis=0, tiled=True)
    rows = jax.ShapeDtypeStruct((BACK, LANES), F32), jax.ShapeDtypeStruct((NEXT, LANES), F32)
    head, tail = call(ends_kernel, rows[::-1], [], 0, 1 << 20, 8, "ends", 1)(plane, recv)
    up = [(z, (z + 1) % planes) for z in range(planes)]
    down = [(t, s) for s, t in up]
    after = lax.ppermute(head, "chan", down)
    before = lax.ppermute(tail, "chan", up)
    flops = 2 * 3 * (2 * HALF * HALF + HOP * 2 * HALF) * LANES
    shared = (specs, forward, back)

    def part(kernel, count, name, scalars, *shapes):
        shapes = tuple(jax.ShapeDtypeStruct(shape, F32) for shape in shapes)
        sums = [pltpu.VMEM((count * MOST + 16, LANES), F32)]
        return call(kernel, shapes, sums, count * flops, 8 << 20, 24, name, scalars)

    middle, own = part(
        near_kernel, 2, "near_segments", 1, (BLOCK, 2 * HOP), (blocks * span, LANES)
    )(plane, recv, *shared)
    early, keep = part(back_kernel, 1, "back_segment", 0, (BLOCK, BACK), (BLOCK, KEEP))(
        own, before, *shared
    )
    given = lax.ppermute(early, "chan", down)
    (last,) = part(last_kernel, 1, "last_segment", 0, (BLOCK, MOST))(own, after, *shared)
    joined = jax.ShapeDtypeStruct((BLOCK, blocks * span), F32)
    return call(join_kernel, joined, [], 0, 1 << 17, 8, "join")(keep, middle, last, given)


def solution(mesh):
    placed = (P(None, ("tmpl", "chan")), P(), P("tmpl", None, None), P(), P())
    return jax.shard_map(
        shards, mesh=mesh, in_specs=placed, out_specs=P("tmpl", "chan"), check_vma=False
    )
```
